1024 devices in a mesh: ctx: 32 (over y_lo, z), head: 16 (over y_hi, x), dp: 2 (over core).
Axes of the slice: x: 4, y: 8 (y_hi: 4, y_lo: 2; y = y_hi * 2 + y_lo), z: 16, core: 2. Of those that a mesh axis runs over, the one named last changes fastest.
Arguments:
- query: bfloat16 [2, 8192, 16384], P('dp', 'ctx', 'head'), may hold values from -4 to 4
- out_grad: bfloat16 [2, 8192, 16384], P('dp', 'ctx', 'head'), may hold values from -6 to 6
- row_lse: float32 [2, 128, 8192], P('dp', 'head', 'ctx'), may hold values from 6 to 8
- row_delta: float32 [2, 128, 8192], P('dp', 'head', 'ctx'), may hold values from -72 to 72
- key_value: bfloat16 [2, 8192, 4096], P('dp', 'ctx', 'head'), may hold values from -9 to 9
- kv_grad_in: float32 [2, 8192, 4096], P('dp', 'ctx', 'head'), may hold values from -1.8 to 1.8
- layer_input: bfloat16 [2, 8192, 8192], P('dp', 'ctx', 'head'), may hold values from -0.119628906 to 0.119628906
- slot_order: int32 [64], replicated, may hold values from 0 to 63, each once
Outputs:
- q_grad: float32 [2, 8192, 16384], P('dp', 'ctx', 'head')
- kv_grad: float32 [2, 8192, 4096], P('dp', 'ctx', 'head')
- v_weight_grad: float32 [16, 512, 2048], P('head', ('ctx', 'dp'))
The draws below stay inside these ranges and needn't reach their ends.
Inputs may be any that keep to these rules, and one draw needn't show every extreme that they name: `slot_order`: A permutation of the slots: every part of 128 tokens of the sequence sits in exactly one slot; device i of ctx holds slots 2i and 2i+1.
All inputs are finite; a program needn't handle non-finite values.
Results may differ from the reference program's by a relative error of at most 0.0037.
Values may be sent and summed in bfloat16 or wider, within the bound.
A program may use at most 32 MiB of HBM per device.

```python
import math
import jax
import jax.numpy as jnp
from jax import lax

DH = 128
HQ = 8
D_WIN = 8192
S_DEV = 256
TOKENS = 8192
SEQS = 2
N_SLOTS = 64
QHEADS = 128
N_CTX = 32
N_HEAD = 16


def with_spikes(values, rng, source, target, shards_of, factor):
    def block_of(dim):
        return (jnp.arange(values.shape[dim]) // (values.shape[dim] // shards_of)).reshape((-1,) + (1,) * (values.ndim - 1 - dim))

    near = jax.random.permutation(rng, shards_of)[block_of(target)]
    second = (block_of(target) + shards_of // 2) % shards_of
    return jnp.where((block_of(source) == near) | (block_of(source) == second), factor * values, values)


def level_of(rng, shape, shards, least, high):
    loudness, own = 1.0, jax.random.fold_in(rng, 6)
    for position, blocks in shards:
        draws = jnp.exp(jax.random.uniform(jax.random.fold_in(own, position), (blocks,), jnp.float32, least / len(shards), high / len(shards)))
        loudness = loudness * jnp.repeat(draws, shape[position] // blocks).reshape([-1 if axis == position else 1 for axis in range(len(shape))])
    return loudness


def bell_draw(rng, shape, deviation, bound, cuts=(), kind=jnp.bfloat16):
    values = deviation * jax.random.normal(rng, shape, jnp.float32)
    if cuts:
        values = values * level_of(rng, shape, cuts, -0.22, 0.18)
    return jnp.clip(values, -bound, bound).astype(kind)


def heavy_noise(stream_key, shape, width, reach, shards, heavy, kind=jnp.bfloat16):
    array = width * jax.random.normal(stream_key, shape, jnp.float32)
    if shards:
        array = array * level_of(stream_key, shape, shards, -0.22, 0.18)
    return jnp.clip(with_spikes(array, jax.random.fold_in(stream_key, 3), *heavy), -reach, reach).astype(kind)


def setup_inputs(seed: int = 0) -> dict:
    streams_of = jax.random.split(jax.random.key(seed), 9)
    query = bell_draw(streams_of[0], (SEQS, TOKENS, QHEADS * DH), 1.0, 4.0, ((0, 2), (1, 32), (2, 16)))
    out_grad = bell_draw(streams_of[1], (SEQS, TOKENS, QHEADS * DH), 1.0, 6.0, ((0, 2), (1, 32), (2, 16)))
    row_lse = jnp.clip(6.0 + 2.0 * jax.random.uniform(streams_of[2], (SEQS, QHEADS, TOKENS), jnp.float32) ** level_of(streams_of[2], (SEQS, QHEADS, TOKENS), ((0, 2), (1, 16), (2, 32)), -0.2, 0.2), 6.0, 8.0)
    row_delta = bell_draw(streams_of[3], (SEQS, QHEADS, TOKENS), 12.0, 72.0, ((0, 2), (1, 16), (2, 32)), jnp.float32)
    key_value = bell_draw(streams_of[4], (SEQS, TOKENS, N_HEAD * 2 * DH), 1.5, 9.0, ((0, 2), (1, 32), (2, 16)))
    kv_grad_in = bell_draw(streams_of[5], (SEQS, TOKENS, N_HEAD * 2 * DH), 0.3, 1.8, ((0, 2), (1, 32), (2, 16)), jnp.float32)
    layer_input = heavy_noise(streams_of[6], (SEQS, TOKENS, D_WIN), 0.02, 0.119628906, ((0, 2), (1, 32), (2, 16)), (1, 2, 32, 2.75))
    slot_order = jax.random.permutation(streams_of[7], N_SLOTS).astype(jnp.int32)
    return {"query": query, "out_grad": out_grad, "row_lse": row_lse, "row_delta": row_delta, "key_value": key_value, "kv_grad_in": kv_grad_in, "layer_input": layer_input, "slot_order": slot_order}


def pair_grads(query_blk, dout_blk, lse_blk, delta_blk, key_rows, value_rows, query_pos, key_pos, softmax_scale):
    query_f = query_blk.astype(jnp.float32)
    dout_f = dout_blk.astype(jnp.float32)
    key_f = key_rows.astype(jnp.float32)
    value_f = value_rows.astype(jnp.float32)
    scores = jnp.einsum('qhd,kd->hqk', query_f, key_f) * softmax_scale
    visible = key_pos[None, None, :] <= query_pos[None, :, None]
    weights = jnp.exp(jnp.where(visible, scores - lse_blk[:, :, None], -1e+30))
    weights_low = weights.astype(jnp.bfloat16)
    value_dots = jnp.einsum('qhd,kd->hqk', dout_f, value_f)
    score_grad = (weights * (value_dots - delta_blk[:, :, None])).astype(jnp.bfloat16)
    score_f = score_grad.astype(jnp.float32)
    query_grad = jnp.einsum('hqk,kd->qhd', score_f, key_f) * softmax_scale
    key_grad = jnp.einsum('hqk,qhd->kd', score_f, query_f) * softmax_scale
    value_part = jnp.einsum('hqk,qhd->kd', weights_low.astype(jnp.float32), dout_f)
    return (query_grad, key_grad, value_part)

def reference(query, out_grad, row_lse, row_delta, key_value, kv_grad_in, layer_input, slot_order):
    half_len = S_DEV // 2
    softmax_scale = 1.0 / math.sqrt(DH)
    positions = (slot_order.reshape(N_CTX, 2)[:, :, None] * half_len + jnp.arange(half_len, dtype=jnp.int32)[None, None, :]).reshape(N_CTX, S_DEV)
    query_out = []
    kv_out = []
    for seq_idx in range(SEQS):

        def one_head(head_idx):
            query_head = lax.dynamic_slice_in_dim(query[seq_idx], head_idx * HQ * DH, HQ * DH, 1).reshape(N_CTX, S_DEV, HQ, DH)
            dout_head = lax.dynamic_slice_in_dim(out_grad[seq_idx], head_idx * HQ * DH, HQ * DH, 1).reshape(N_CTX, S_DEV, HQ, DH)
            lse_head = lax.dynamic_slice_in_dim(row_lse[seq_idx], head_idx * HQ, HQ, 0).reshape(HQ, N_CTX, S_DEV)
            delta_head = lax.dynamic_slice_in_dim(row_delta[seq_idx], head_idx * HQ, HQ, 0).reshape(HQ, N_CTX, S_DEV)
            kv_head = lax.dynamic_slice_in_dim(key_value[seq_idx], head_idx * 2 * DH, 2 * DH, 1).reshape(N_CTX, S_DEV, 2 * DH)
            kvin_head = lax.dynamic_slice_in_dim(kv_grad_in[seq_idx], head_idx * 2 * DH, 2 * DH, 1).reshape(N_CTX, S_DEV, 2 * DH)

            def one_block(block_idx):
                left_block = (block_idx + N_CTX - 1) % N_CTX
                right_block = (block_idx + 1) % N_CTX
                kv_both = jnp.concatenate([kv_head[left_block], kv_head[right_block]], axis=0)
                key_pos = jnp.concatenate([positions[left_block], positions[right_block]], axis=0)
                query_grad, key_grad, value_part = pair_grads(query_head[block_idx], dout_head[block_idx], lse_head[:, block_idx], delta_head[:, block_idx], kv_both[:, :DH], kv_both[:, DH:], positions[block_idx], key_pos, softmax_scale)
                return (query_grad.reshape(S_DEV, HQ * DH), jnp.concatenate([key_grad, value_part], axis=1))
            query_all, partial_all = lax.map(one_block, jnp.arange(N_CTX, dtype=jnp.int32))
            to_left = partial_all[:, :S_DEV]
            to_right = partial_all[:, S_DEV:]
            kv_new = kvin_head + jnp.roll(to_left, -1, axis=0) + jnp.roll(to_right, 1, axis=0)
            return (query_all.reshape(TOKENS, HQ * DH), kv_new.reshape(TOKENS, 2 * DH))
        query_heads, kv_heads = lax.map(one_head, jnp.arange(N_HEAD, dtype=jnp.int32))
        query_out.append(jnp.transpose(query_heads, (1, 0, 2)).reshape(TOKENS, N_HEAD * HQ * DH))
        kv_out.append(jnp.transpose(kv_heads, (1, 0, 2)).reshape(TOKENS, N_HEAD * 2 * DH))
    q_grad = jnp.stack(query_out, axis=0)
    kv_grad = jnp.stack(kv_out, axis=0)
    value_grad = kv_grad.reshape(SEQS, TOKENS, N_HEAD, 2, DH)[:, :, :, 1, :].reshape(SEQS, TOKENS, N_HEAD * DH).astype(jnp.bfloat16)
    summed = jnp.zeros((D_WIN, N_HEAD * DH), jnp.float32)
    for seq_idx in range(SEQS):
        summed = summed + jnp.dot(layer_input[seq_idx].T, value_grad[seq_idx], preferred_element_type=jnp.float32)
    return (q_grad, kv_grad, summed.reshape(N_HEAD, D_WIN // N_HEAD, N_HEAD * DH))
```

```python
import functools
import math

import jax
import jax.numpy as jnp
from jax import lax
from jax.experimental import pallas as pl
from jax.experimental.pallas import tpu as pltpu
from jax.sharding import PartitionSpec as P

MESH = pl.DeviceIdType.MESH
LOG2E = 1.0 / math.log(2.0)
NYH = 4


def nt(a, b):
    return lax.dot_general(a, b, (((1,), (1,)), ((), ())), preferred_element_type=jnp.float32)


def tn(a, b):
    return lax.dot_general(a, b, (((0,), (0,)), ((), ())), preferred_element_type=jnp.float32)


def nn(a, b):
    return lax.dot_general(a, b, (((1,), (0,)), ((), ())), preferred_element_type=jnp.float32)


def kernel(
    nctx, nx,
    slots, q, do, lse, delta, kv, kvin, feats,
    qg, kvg, wg,
    kb, vb, prob, dv, dk, rdv, rdk, lt, vgb, vall, acc, rp, rm, fin, gat, lrow,
    s_kv, r_kv, s_part, r_part, s_l, r_l, r_core, s_v, r_v, s_p, r_p, s_m, r_m, s_f, r_f,
):
    ctx, head, p = lax.axis_index("ctx"), lax.axis_index("head"), lax.axis_index("dp")
    nz = nctx // 2
    np_, nm = nz // 2, nz - 1 - nz // 2
    e, z = ctx // nz, ctx % nz
    yh, x = head // nx, head % nx
    S, dh = kb.shape[1], kb.shape[2]
    half = S // 2
    hq = q.shape[1] // dh
    F = feats.shape[1]
    scale = 1.0 / math.sqrt(dh)
    left, right = (ctx + nctx - 1) % nctx, (ctx + 1) % nctx
    mine = 2 * e + p
    xs = [(x + r) % nx for r in range(nx)]

    def dev(c=ctx, h=head, d=p):
        return (c, h, d)

    def at(e_=e, z_=z, y_=yh, x_=x, p_=p):
        return (e_ * nz + z_, y_ * nx + x_, p_)

    def send(src, dst, ss, rs, to):
        copy = pltpu.make_async_remote_copy(
            src_ref=src, dst_ref=dst, send_sem=ss, recv_sem=rs, device_id=to, device_id_type=MESH
        )
        copy.start()
        return copy

    def arrived(dst, rs):
        pltpu.make_async_remote_copy(
            src_ref=dst, dst_ref=dst, send_sem=rs, recv_sem=rs, device_id=dev(d=1 - p), device_id_type=MESH
        ).wait_recv()

    barrier = pltpu.get_barrier_semaphore()

    def greet(to):
        pl.semaphore_signal(barrier, inc=1, device_id=to, device_id_type=MESH)

    greet(dev(c=left))
    greet(dev(c=right))
    greet(at(z_=(z + 1) % nz))
    greet(at(z_=(z + nz - 1) % nz))
    group = [(r, a, b) for r in range(nx) for a in (0, 1) for b in (0, 1) if (r, a, b) != (0, 0, 0)]

    def member(r, a, b):
        return (1 - e if a else e), xs[r], (1 - p if b else p)

    for r, a, b in group:
        e_, x_, p_ = member(r, a, b)
        greet(at(e_=e_, x_=x_, p_=p_))

    @pl.when(mine != yh)
    def _():
        for e_ in (0, 1):
            for p_ in (0, 1):
                greet(at(e_=e_, y_=mine, p_=p_))

    pl.semaphore_wait(barrier, 4 + len(group) + NYH - 1)

    sends = []
    for part, buf in ((0, kb), (1, vb)):
        cols = slice(part * dh, (part + 1) * dh)
        for side, to in ((0, right), (1, left)):
            sends.append(send(kv.at[:, cols], buf.at[side], s_kv.at[part, side], r_kv.at[part, side], dev(c=to)))

    lt[x, e, p] = feats[...].T
    own = lt.at[x, e, p]
    sends.append(send(own, own, s_l.at[0], r_l.at[0], at(e_=1 - e)))
    if nx > 1:
        xp, xm, xo = xs[1], xs[nx - 1], xs[2]
        sends.append(send(own, own, s_l.at[1], r_l.at[1], at(x_=xp)))
        sends.append(send(own, own, s_l.at[2], r_l.at[3], at(x_=xm)))
    sends.append(send(own, own, s_l.at[3], r_core.at[0], at(p_=1 - p)))

    for side, blk in ((0, left), (1, right)):
        for kh in (0, 1):
            for qh in (0, 1):
                hidden = jnp.where(slots[2 * blk + kh] < slots[2 * ctx + qh], 0.0, 1e30).astype(jnp.float32)
                lanes = slice(qh * half, (qh + 1) * half)
                lrow[side, kh, :, lanes] = lse[:, lanes] * LOG2E + hidden

    for side, to in ((0, left), (1, right)):
        arrived(kb.at[side], r_kv.at[0, side])
        dv[side] = jnp.zeros((S, dh), jnp.float32)

        def value_step(m, carry, side=side):
            lanes = pl.ds(pl.multiple_of(m * dh, dh), dh)
            st = nt(kb[side], q[:, lanes]) * (scale * LOG2E)
            st = st.reshape(2, half, S) - lrow[side, :, pl.ds(m, 1), :]
            pr = jnp.exp2(st).reshape(S, S)
            prob[m, side] = pr
            dv[side] += nn(pr.astype(jnp.bfloat16), do[:, lanes])
            return carry

        lax.fori_loop(0, hq, value_step, 0)
        sends.append(send(dv.at[side], rdv.at[side], s_part.at[0, side], r_part.at[0, side], dev(c=to)))

    dk[...] = jnp.zeros(dk.shape, jnp.float32)
    for side in (0, 1):
        arrived(vb.at[side], r_kv.at[1, side])

    def rest_step(m, carry):
        lanes = pl.ds(pl.multiple_of(m * dh, dh), dh)
        qm, dom = q[:, lanes], do[:, lanes]
        total = None
        for side in (0, 1):
            dots = nt(vb[side], dom) - delta[pl.ds(m, 1), :]
            ds = (prob[m, side] * dots).astype(jnp.bfloat16)
            dk[side] += nn(ds, qm)
            term = tn(ds, kb[side])
            total = term if total is None else total + term
        qg[:, lanes] = total * scale
        return carry

    lax.fori_loop(0, hq, rest_step, 0)
    for side, to in ((0, left), (1, right)):
        dk[side] = dk[side] * scale
        sends.append(send(dk.at[side], rdk.at[side], s_part.at[1, side], r_part.at[1, side], dev(c=to)))

    for side in (0, 1):
        arrived(rdv.at[side], r_part.at[0, side])
    new_v = kvin[:, dh:] + rdv[0] + rdv[1]
    kvg[:, dh:] = new_v
    vgb[...] = new_v.astype(jnp.bfloat16)
    te, tp = yh // 2, yh % 2
    for o in range(1, NYH):
        sends.append(send(vgb, vall.at[e, p], s_v.at[o], r_v.at[e, p], at(e_=te, y_=(yh + o) % NYH, p_=tp)))

    @pl.when(mine == yh)
    def _():
        vall[e, p] = vgb[...]

    @pl.when(mine != yh)
    def _():
        send(vgb, vall.at[e, p], s_v.at[0], r_v.at[e, p], at(e_=te, p_=tp))

    n_l = 4
    core = 1

    def pass_on(ref, sem, to):
        nonlocal n_l
        sends.append(send(ref, ref, s_l.at[n_l], sem, to))
        n_l += 1

    other = lt.at[x, 1 - e, p]
    arrived(other, r_l.at[0])
    if nx > 1:
        pass_on(other, r_l.at[2], at(x_=xp))
        pass_on(other, r_l.at[4], at(x_=xm))
    pass_on(other, r_core.at[1], at(p_=1 - p))
    hf = F // 2
    if nx > 1:
        for a in (0, 1):
            e_ = 1 - e if a else e
            low = lt.at[xm, e_, p]
            arrived(low, r_l.at[1 + a])
            pass_on(low.at[:hf], r_l.at[5 + a], at(x_=xp))
            pass_on(low, r_core.at[2 + a], at(p_=1 - p))
            high = lt.at[xp, e_, p]
            arrived(high, r_l.at[3 + a])
            pass_on(high.at[hf:], r_l.at[7 + a], at(x_=xm))
            pass_on(high, r_core.at[4 + a], at(p_=1 - p))

    for side in (0, 1):
        arrived(rdk.at[side], r_part.at[1, side])
    kvg[:, :dh] = kvin[:, :dh] + rdk[0] + rdk[1]

    for e_ in (0, 1):
        for p_ in (0, 1):
            @pl.when((mine != yh) | (e_ != e) | (p_ != p))
            def _(e_=e_, p_=p_):
                arrived(vall.at[e_, p_], r_v.at[e_, p_])

    zp, zm = at(z_=(z + 1) % nz), at(z_=(z + nz - 1) % nz)

    def up(step, r, src):
        return send(src, rp.at[step, r], s_p.at[step, r], r_p.at[step, r], zp)

    def down(step, r, src):
        return send(src, rm.at[step, r], s_m.at[step, r], r_m.at[step, r], zm)

    def weight_term(r, sems):
        for i in sems:
            k, a = i
            e_ = 1 - e if a else e
            arrived(lt.at[xs[r], e_, 1 - p], r_core.at[k])
        total = None
        for e_ in (0, 1):
            for p_ in (0, 1):
                term = nn(lt[xs[r], e_, p_], vall[e_, p_])
                total = term if total is None else total + term
        acc[r] = total.reshape(acc.shape[1:])
        up(0, r, acc.at[r, :, (z + np_) % nz])
        if nm:
            down(0, r, acc.at[r, :, (z + nz - nm) % nz])

    weight_term(0, ((0, 0), (1, 1)))
    if nx > 1:
        weight_term(nx - 1, ((2, 0), (3, 1)))
        weight_term(1, ((4, 0), (5, 1)))
        for a in (0, 1):
            e_ = 1 - e if a else e
            far = lt.at[xo, e_, p]
            arrived(far.at[:hf], r_l.at[5 + a])
            arrived(far.at[hf:], r_l.at[7 + a])
            pass_on(far, r_core.at[6 + a], at(p_=1 - p))
        weight_term(2, ((6, 0), (7, 1)))
    order = (0, nx - 1, 1, 2) if nx > 1 else (0,)

    def chain(step, both):
        for r in order:
            arrived(rp.at[step, r], r_p.at[step, r])
            rp[step, r] += acc[r, :, (z + np_ - 1 - step) % nz]
            up(step + 1, r, rp.at[step, r])
            if both:
                arrived(rm.at[step, r], r_m.at[step, r])
                rm[step, r] += acc[r, :, (z + nz - nm + 1 + step) % nz]
                down(step + 1, r, rm.at[step, r])

    def chain_step(step, carry):
        chain(step, True)
        return carry

    if nm > 1:
        lax.fori_loop(0, nm - 1, chain_step, 0)
    for step in range(max(nm - 1, 0), np_ - 1):
        chain(step, False)

    for r in order:
        whole = acc[r, :, z]
        arrived(rp.at[np_ - 1, r], r_p.at[np_ - 1, r])
        whole = whole + rp[np_ - 1, r]
        if nm:
            arrived(rm.at[nm - 1, r], r_m.at[nm - 1, r])
            whole = whole + rm[nm - 1, r]
        fin[r] = whole.reshape(fin.shape[1:])
        for i, (r_, a, b) in enumerate(group):
            if r_ == r:
                e_, x_, p_ = member(r, a, b)
                col = mine * nx + x
                sends.append(
                    send(fin.at[r, e_, p_], gat.at[col], s_f.at[i], r_f.at[r, a, b], at(e_=e_, x_=x_, p_=p_))
                )
    gat[mine * nx + x] = fin[0, e, p]
    for r, a, b in group:
        e_, _, p_ = member(r, a, b)
        col = (2 * e_ + p_) * nx + xs[(nx - r) % nx]
        arrived(gat.at[col], r_f.at[r, a, b])
    for c in range(NYH * nx):
        wg[:, c * dh : (c + 1) * dh] = gat[c]

    for copy in sends:
        copy.wait_send()

    @pl.when(mine != yh)
    def _():
        pltpu.make_async_remote_copy(
            src_ref=vgb, dst_ref=vall.at[e, p], send_sem=s_v.at[0], recv_sem=r_v.at[e, p],
            device_id=at(e_=te, p_=tp), device_id_type=MESH,
        ).wait_send()

    def left_(src, ss):
        pltpu.make_async_remote_copy(
            src_ref=src, dst_ref=src, send_sem=ss, recv_sem=ss, device_id=zp, device_id_type=MESH
        ).wait_send()

    for r in order:
        left_(acc.at[r, :, 0], s_p.at[0, r])
        if nm:
            left_(acc.at[r, :, 0], s_m.at[0, r])

    def drain(step, carry):
        for r in order:
            left_(rp.at[0, r], s_p.at[step, r])
        return carry

    def drain_m(step, carry):
        for r in order:
            left_(rm.at[0, r], s_m.at[step, r])
        return carry

    lax.fori_loop(1, np_, drain, 0)
    if nm > 1:
        lax.fori_loop(1, nm, drain_m, 0)


def on_device(nctx, nx, query, out_grad, row_lse, row_delta, key_value, kv_grad_in, layer_input, slot_order):
    S, dh = query.shape[1], key_value.shape[2] // 2
    hq = query.shape[2] // dh
    F = layer_input.shape[2]
    nz = nctx // 2
    rows = F // (2 * nctx)
    np_, nm = nz // 2, max(nz - 1 - nz // 2, 1)
    f32, bf16 = jnp.float32, jnp.bfloat16
    vmem = pl.BlockSpec(memory_space=pltpu.VMEM)
    dma = pltpu.SemaphoreType.DMA
    piece = (nx, 2, 2 * rows, dh)
    outs = pl.pallas_call(
        functools.partial(kernel, nctx, nx),
        out_shape=(
            jax.ShapeDtypeStruct((S, hq * dh), f32),
            jax.ShapeDtypeStruct((S, 2 * dh), f32),
            jax.ShapeDtypeStruct((rows, NYH * nx * dh), f32),
        ),
        in_specs=[pl.BlockSpec(memory_space=pltpu.SMEM)] + [vmem] * 7,
        out_specs=(vmem,) * 3,
        scratch_shapes=[
            pltpu.VMEM((2, S, dh), bf16),
            pltpu.VMEM((2, S, dh), bf16),
            pltpu.VMEM((hq, 2, S, S), f32),
            pltpu.VMEM((2, S, dh), f32),
            pltpu.VMEM((2, S, dh), f32),
            pltpu.VMEM((2, S, dh), f32),
            pltpu.VMEM((2, S, dh), f32),
            pltpu.VMEM((nx, 2, 2, F, S), bf16),
            pltpu.VMEM((S, dh), bf16),
            pltpu.VMEM((2, 2, S, dh), bf16),
            pltpu.VMEM((nx, 2, nz, 2 * rows, dh), f32),
            pltpu.VMEM((np_,) + piece, f32),
            pltpu.VMEM((nm,) + piece, f32),
            pltpu.VMEM((nx, 2, 2, rows, dh), f32),
            pltpu.VMEM((NYH * nx, rows, dh), f32),
            pltpu.VMEM((2, 2, hq, S), f32),
            dma((2, 2)), dma((2, 2)), dma((2, 2)), dma((2, 2)),
            dma((20,)), dma((9,)), dma((8,)),
            dma((4,)), dma((2, 2)),
            dma((np_, nx)), dma((np_, nx)), dma((nm, nx)), dma((nm, nx)),
            dma((16,)), dma((nx, 2, 2)),
        ],
        compiler_params=pltpu.CompilerParams(
            collective_id=0, has_side_effects=True, vmem_limit_bytes=48 * 1024 * 1024
        ),
        cost_estimate=pl.CostEstimate(flops=2_000_000_000, bytes_accessed=6_000_000, transcendentals=1_000_000),
    )(
        slot_order, query[0], out_grad[0], row_lse[0], row_delta[0], key_value[0], kv_grad_in[0], layer_input[0]
    )
    return outs[0][None], outs[1][None], outs[2][None]


def solution(mesh):
    nctx, nhead = mesh.shape["ctx"], mesh.shape["head"]
    in_specs = (
        P("dp", "ctx", "head"),
        P("dp", "ctx", "head"),
        P("dp", "head", "ctx"),
        P("dp", "head", "ctx"),
        P("dp", "ctx", "head"),
        P("dp", "ctx", "head"),
        P("dp", "ctx", "head"),
        P(),
    )
    out_specs = (P("dp", "ctx", "head"), P("dp", "ctx", "head"), P("head", ("ctx", "dp"), None))
    return jax.shard_map(
        functools.partial(on_device, nctx, nhead // NYH),
        mesh=mesh, in_specs=in_specs, out_specs=out_specs, check_vma=False,
    )
```

```python
import functools
import math

import jax
import jax.numpy as jnp
from jax import lax
from jax.experimental import pallas as pl
from jax.experimental.pallas import tpu as pltpu
from jax.sharding import PartitionSpec as P

MESH = pl.DeviceIdType.MESH
LOG2E = 1.0 / math.log(2.0)
NYH = 4


def nt(a, b):
    return lax.dot_general(a, b, (((1,), (1,)), ((), ())), preferred_element_type=jnp.float32)


def tn(a, b):
    return lax.dot_general(a, b, (((0,), (0,)), ((), ())), preferred_element_type=jnp.float32)


def nn(a, b):
    return lax.dot_general(a, b, (((1,), (0,)), ((), ())), preferred_element_type=jnp.float32)


def kernel(
    nctx, nx,
    slots, q_h, do_h, lse_h, delta_h, kv, kvin_h, feats_h,
    qg, kvg, wg,
    q, do, lse, delta, kvin, feats, kb, vb, prob, dv, dk, rdv, rdk, lt, vgb, vall, acc, odd_out, odd_in, even_out, even_in, fin, gat, lrow,
    s_in, s_kv, r_kv, s_part, r_part, s_l, r_l, r_core, s_v, r_v, s_odd, r_odd, s_even, r_even, s_f, r_f,
):
    ctx, head, p = lax.axis_index("ctx"), lax.axis_index("head"), lax.axis_index("dp")
    nz = nctx // 2
    np_ = nz // 2
    e, z = ctx // nz, ctx % nz
    yh, x = head // nx, head % nx
    S, dh = kb.shape[1], kb.shape[2]
    half = S // 2
    hq = q.shape[1] // dh
    F = feats.shape[1]
    scale = 1.0 / math.sqrt(dh)
    left, right = (ctx + nctx - 1) % nctx, (ctx + 1) % nctx
    mine = 2 * e + p
    xs = [(x + r) % nx for r in range(nx)]

    def dev(c=ctx, h=head, d=p):
        return (c, h, d)

    def at(e_=e, z_=z, y_=yh, x_=x, p_=p):
        return (e_ * nz + z_, y_ * nx + x_, p_)

    def send(src, dst, ss, rs, to):
        copy = pltpu.make_async_remote_copy(
            src_ref=src, dst_ref=dst, send_sem=ss, recv_sem=rs, device_id=to, device_id_type=MESH
        )
        copy.start()
        return copy

    def arrived(dst, rs):
        pltpu.make_async_remote_copy(
            src_ref=dst, dst_ref=dst, send_sem=rs, recv_sem=rs, device_id=dev(d=1 - p), device_id_type=MESH
        ).wait_recv()

    fetched = [
        pltpu.make_async_copy(src, dst, s_in.at[i])
        for i, (src, dst) in enumerate(
            ((feats_h, feats), (lse_h, lse), (q_h, q), (do_h, do), (delta_h, delta), (kvin_h, kvin))
        )
    ]
    for copy in fetched:
        copy.start()

    barrier = pltpu.get_barrier_semaphore()

    def greet(to):
        pl.semaphore_signal(barrier, inc=1, device_id=to, device_id_type=MESH)

    greet(dev(c=left))
    greet(dev(c=right))
    greet(at(z_=(z + 1) % nz))
    greet(at(z_=(z + nz - 1) % nz))
    greet(at(z_=(z + 2) % nz))
    greet(at(z_=(z + nz - 2) % nz))
    group = [(r, a, b) for r in range(nx) for a in (0, 1) for b in (0, 1) if (r, a, b) != (0, 0, 0)]

    def member(r, a, b):
        return (1 - e if a else e), xs[r], (1 - p if b else p)

    for r, a, b in group:
        e_, x_, p_ = member(r, a, b)
        greet(at(e_=e_, x_=x_, p_=p_))

    @pl.when(mine != yh)
    def _():
        for e_ in (0, 1):
            for p_ in (0, 1):
                greet(at(e_=e_, y_=mine, p_=p_))

    pl.semaphore_wait(barrier, 6 + len(group) + NYH - 1)

    sends = []
    for part, buf in ((0, kb), (1, vb)):
        cols = slice(part * dh, (part + 1) * dh)
        for side, to in ((0, right), (1, left)):
            sends.append(send(kv.at[:, cols], buf.at[side], s_kv.at[part, side], r_kv.at[part, side], dev(c=to)))

    fetched[0].wait()
    lt[x, e, p] = feats[...].T
    own = lt.at[x, e, p]
    hf = F // 2
    passed = []

    def pass_on(ref, sem, to):
        passed.append(send(ref, ref, s_l.at[len(passed)], sem, to))

    to_core = at(p_=1 - p)
    pass_on(own, r_l.at[0], at(e_=1 - e))
    if nx > 1:
        xp, xm, xo = xs[1], xs[nx - 1], xs[2]
        pass_on(own, r_l.at[1], at(x_=xp))
        pass_on(own, r_l.at[3], at(x_=xm))
    pass_on(own, r_core.at[0, 0], to_core)

    def share_other():
        other = lt.at[x, 1 - e, p]
        arrived(other, r_l.at[0])
        if nx > 1:
            pass_on(other, r_l.at[2], at(x_=xp))
            pass_on(other, r_l.at[4], at(x_=xm))
        pass_on(other, r_core.at[0, 1], to_core)

    def share_side(a):
        if nx > 1:
            e_ = 1 - e if a else e
            low, high = lt.at[xm, e_, p], lt.at[xp, e_, p]
            arrived(low, r_l.at[1 + a])
            pass_on(low.at[:hf], r_l.at[5 + a], at(x_=xp))
            arrived(high, r_l.at[3 + a])
            pass_on(high.at[hf:], r_l.at[7 + a], at(x_=xm))
            pass_on(low, r_core.at[nx - 1, a], to_core)
            pass_on(high, r_core.at[1, a], to_core)

    def share_far(a):
        if nx > 1:
            far = lt.at[xo, 1 - e if a else e, p]
            arrived(far.at[:hf], r_l.at[5 + a])
            arrived(far.at[hf:], r_l.at[7 + a])
            pass_on(far, r_core.at[2, a], to_core)

    for copy in fetched[1:4]:
        copy.wait()

    for side, blk in ((0, left), (1, right)):
        for kh in (0, 1):
            for qh in (0, 1):
                hidden = jnp.where(slots[2 * blk + kh] < slots[2 * ctx + qh], 0.0, 1e30).astype(jnp.float32)
                lanes = slice(qh * half, (qh + 1) * half)
                lrow[side, kh, :, lanes] = lse[:, lanes] * LOG2E + hidden

    heads = [slice(m * dh, (m + 1) * dh) for m in range(hq)]
    for side, to in ((0, left), (1, right)):
        arrived(kb.at[side], r_kv.at[0, side])
        total = None
        for m, lanes in enumerate(heads):
            st = nt(kb[side], q[:, lanes]) * (scale * LOG2E)
            st = st.reshape(2, half, S) - lrow[side, :, m : m + 1, :]
            pr = jnp.exp2(st).reshape(S, S)
            prob[m, side] = pr
            term = nn(pr.astype(jnp.bfloat16), do[:, lanes])
            total = term if total is None else total + term
        dv[side] = total
        sends.append(send(dv.at[side], rdv.at[side], s_part.at[0, side], r_part.at[0, side], dev(c=to)))

    share_other()

    for copy in fetched[4:]:
        copy.wait()
    for side in (0, 1):
        arrived(vb.at[side], r_kv.at[1, side])
    totals = [None, None]
    for m, lanes in enumerate(heads):
        qm, dom = q[:, lanes], do[:, lanes]
        whole = None
        for side in (0, 1):
            dots = nt(vb[side], dom) - delta[m : m + 1, :]
            ds = (prob[m, side] * dots).astype(jnp.bfloat16)
            term = nn(ds, qm)
            totals[side] = term if totals[side] is None else totals[side] + term
            term = tn(ds, kb[side])
            whole = term if whole is None else whole + term
        qg[:, lanes] = whole
    for side, to in ((0, left), (1, right)):
        dk[side] = totals[side] * scale
        sends.append(send(dk.at[side], rdk.at[side], s_part.at[1, side], r_part.at[1, side], dev(c=to)))

    share_side(0)

    for side in (0, 1):
        arrived(rdv.at[side], r_part.at[0, side])
    new_v = kvin[:, dh:] + rdv[0] + rdv[1]
    kvg[:, dh:] = new_v
    vgb[...] = new_v.astype(jnp.bfloat16)
    te, tp = yh // 2, yh % 2
    for o in range(1, NYH):
        sends.append(send(vgb, vall.at[e, p], s_v.at[o], r_v.at[e, p], at(e_=te, y_=(yh + o) % NYH, p_=tp)))

    @pl.when(mine == yh)
    def _():
        vall[e, p] = vgb[...]

    @pl.when(mine != yh)
    def _():
        send(vgb, vall.at[e, p], s_v.at[0], r_v.at[e, p], at(e_=te, p_=tp))

    share_far(0)
    share_side(1)

    for side in (0, 1):
        arrived(rdk.at[side], r_part.at[1, side])
    kvg[:, :dh] = kvin[:, :dh] + rdk[0] + rdk[1]

    for e_ in (0, 1):
        for p_ in (0, 1):
            @pl.when((mine != yh) | (e_ != e) | (p_ != p))
            def _(e_=e_, p_=p_):
                arrived(vall.at[e_, p_], r_v.at[e_, p_])

    order = (0, nx - 1, 1, 2) if nx > 1 else (0,)
    ng = odd_in.shape[2]
    per = len(order) // ng
    kc = np_ // 2

    def blocks(g):
        return slice(g * per, (g + 1) * per)

    def term_for(g, d, k):
        to = (z + k) % nz if d == 0 else (z + nz - k) % nz
        return acc[blocks(g), :, to]

    def weight_term(i):
        r = order[i]
        for a in (0, 1):
            e_, x_, _ = member(r, a, 0)
            arrived(lt.at[x_, e_, 1 - p], r_core.at[r, a])
        total = None
        for e_ in (0, 1):
            for p_ in (0, 1):
                term = nn(lt[xs[r], e_, p_], vall[e_, p_])
                total = term if total is None else total + term
        acc[i] = total.reshape(acc.shape[1:])

    def next_odd(i, g, d):
        k = np_ - 1 - 2 * i
        odd_out[d, i, g] = term_for(g, d, k).astype(jnp.bfloat16)
        sends.append(send(odd_out.at[d, i, g], odd_in.at[d, i, g], s_odd.at[d, i, g], r_odd.at[d, i, g], beside[d]))

    def stop(i, g, d):
        k = np_ - 2 * i - (0 if d == 0 else 2)
        value = term_for(g, d, k)
        got = i - 1 if d == 0 else i
        if got >= 0:
            arrived(odd_in.at[d, got, g], r_odd.at[d, got, g])
            value = value + odd_in[d, got, g].astype(jnp.float32)
        if i > 0:
            arrived(even_in.at[d, i - 1, g], r_even.at[d, i - 1, g])
            value = value + even_in[d, i - 1, g].astype(jnp.float32)
        even_out[d, i, g] = value.astype(jnp.bfloat16)
        sends.append(
            send(even_out.at[d, i, g], even_in.at[d, i, g], s_even.at[d, i, g], r_even.at[d, i, g], beyond[d])
        )

    beside = (at(z_=(z + 1) % nz), at(z_=(z + nz - 1) % nz))
    beyond = (at(z_=(z + 2) % nz), at(z_=(z + nz - 2) % nz))
    for g in range(ng):
        if per == 2 and g == 1:
            share_far(1)
        for i in range(g * per, (g + 1) * per):
            weight_term(i)
        stop(0, g, 0)
        for i in range(kc):
            next_odd(i, g, 1)
            next_odd(i, g, 0)
    for i in range(kc):
        for g in range(ng):
            if i > 0:
                stop(i, g, 0)
            if i < kc - 1:
                stop(i, g, 1)

    for i, r in enumerate(order):
        g, k = i // per, i % per
        whole = acc[i, :, z]
        for d, n in ((0, kc), (1, kc - 1)):
            if k == 0:
                arrived(odd_in.at[d, kc - 1, g], r_odd.at[d, kc - 1, g])
            whole = whole + odd_in[d, kc - 1, g, k].astype(jnp.float32)
            if n > 0:
                if k == 0:
                    arrived(even_in.at[d, n - 1, g], r_even.at[d, n - 1, g])
                whole = whole + even_in[d, n - 1, g, k].astype(jnp.float32)
        fin[r] = whole.reshape(fin.shape[1:])
        for j, (r_, a, b) in enumerate(group):
            if r_ == r:
                e_, x_, p_ = member(r, a, b)
                col = mine * nx + x
                sends.append(
                    send(fin.at[r, e_, p_], gat.at[col], s_f.at[j], r_f.at[r, a, b], at(e_=e_, x_=x_, p_=p_))
                )
    gat[mine * nx + x] = fin[0, e, p]
    for r, a, b in group:
        e_, _, p_ = member(r, a, b)
        col = (2 * e_ + p_) * nx + xs[(nx - r) % nx]
        arrived(gat.at[col], r_f.at[r, a, b])
    for c in range(NYH * nx):
        wg[:, c * dh : (c + 1) * dh] = gat[c]

    for copy in sends + passed:
        copy.wait_send()

    @pl.when(mine != yh)
    def _():
        pltpu.make_async_remote_copy(
            src_ref=vgb, dst_ref=vall.at[e, p], send_sem=s_v.at[0], recv_sem=r_v.at[e, p],
            device_id=at(e_=te, p_=tp), device_id_type=MESH,
        ).wait_send()


def on_device(nctx, nx, query, out_grad, row_lse, row_delta, key_value, kv_grad_in, layer_input, slot_order):
    S, dh = query.shape[1], key_value.shape[2] // 2
    hq = query.shape[2] // dh
    F = layer_input.shape[2]
    nz = nctx // 2
    rows = F // (2 * nctx)
    kc = nz // 4
    f32, bf16 = jnp.float32, jnp.bfloat16
    vmem = pl.BlockSpec(memory_space=pltpu.VMEM)
    dma = pltpu.SemaphoreType.DMA
    ng = 2 if nx > 1 else 1
    piece = (ng, nx // ng, 2, 2 * rows, dh)
    outs = pl.pallas_call(
        functools.partial(kernel, nctx, nx),
        out_shape=(
            jax.ShapeDtypeStruct((S, hq * dh), f32),
            jax.ShapeDtypeStruct((S, 2 * dh), f32),
            jax.ShapeDtypeStruct((rows, NYH * nx * dh), f32),
        ),
        in_specs=[pl.BlockSpec(memory_space=pltpu.SMEM)] + [pl.BlockSpec(memory_space=pl.ANY)] * 7,
        out_specs=(vmem,) * 3,
        scratch_shapes=[
            pltpu.VMEM((S, hq * dh), bf16),
            pltpu.VMEM((S, hq * dh), bf16),
            pltpu.VMEM((hq, S), f32),
            pltpu.VMEM((hq, S), f32),
            pltpu.VMEM((S, 2 * dh), f32),
            pltpu.VMEM((S, F), bf16),
            pltpu.VMEM((2, S, dh), bf16),
            pltpu.VMEM((2, S, dh), bf16),
            pltpu.VMEM((hq, 2, S, S), f32),
            pltpu.VMEM((2, S, dh), f32),
            pltpu.VMEM((2, S, dh), f32),
            pltpu.VMEM((2, S, dh), f32),
            pltpu.VMEM((2, S, dh), f32),
            pltpu.VMEM((nx, 2, 2, F, S), bf16),
            pltpu.VMEM((S, dh), bf16),
            pltpu.VMEM((2, 2, S, dh), bf16),
            pltpu.VMEM((nx, 2, nz, 2 * rows, dh), f32),
            pltpu.VMEM((2, kc) + piece, bf16),
            pltpu.VMEM((2, kc) + piece, bf16),
            pltpu.VMEM((2, kc) + piece, bf16),
            pltpu.VMEM((2, kc) + piece, bf16),
            pltpu.VMEM((nx, 2, 2, rows, dh), f32),
            pltpu.VMEM((NYH * nx, rows, dh), f32),
            pltpu.VMEM((2, 2, hq, S), f32),
            dma((6,)), dma((2, 2)), dma((2, 2)), dma((2, 2)), dma((2, 2)),
            dma((20,)), dma((9,)), dma((nx, 2)),
            dma((4,)), dma((2, 2)),
            dma((2, kc, ng)), dma((2, kc, ng)), dma((2, kc, ng)), dma((2, kc, ng)),
            dma((16,)), dma((nx, 2, 2)),
        ],
        compiler_params=pltpu.CompilerParams(
            collective_id=0, has_side_effects=True, vmem_limit_bytes=58 * 1024 * 1024
        ),
        cost_estimate=pl.CostEstimate(flops=2_000_000_000, bytes_accessed=6_000_000, transcendentals=1_000_000),
    )(
        slot_order, query[0], out_grad[0], row_lse[0], row_delta[0], key_value[0], kv_grad_in[0], layer_input[0]
    )
    return (outs[0] * (1.0 / math.sqrt(dh)))[None], outs[1][None], outs[2][None]


def solution(mesh):
    nctx, nhead = mesh.shape["ctx"], mesh.shape["head"]
    in_specs = (
        P("dp", "ctx", "head"),
        P("dp", "ctx", "head"),
        P("dp", "head", "ctx"),
        P("dp", "head", "ctx"),
        P("dp", "ctx", "head"),
        P("dp", "ctx", "head"),
        P("dp", "ctx", "head"),
        P(),
    )
    out_specs = (P("dp", "ctx", "head"), P("dp", "ctx", "head"), P("head", ("ctx", "dp"), None))
    return jax.shard_map(
        functools.partial(on_device, nctx, nhead // NYH),
        mesh=mesh, in_specs=in_specs, out_specs=out_specs, check_vma=False,
    )
```

```python
import functools
import math

import jax
import jax.numpy as jnp
from jax import lax
from jax.experimental import pallas as pl
from jax.experimental.pallas import tpu as pltpu
from jax.sharding import PartitionSpec as P

MESH = pl.DeviceIdType.MESH
LOG2E = 1.0 / math.log(2.0)
NYH = 4


def nt(a, b):
    return lax.dot_general(a, b, (((1,), (1,)), ((), ())), preferred_element_type=jnp.float32)


def tn(a, b):
    return lax.dot_general(a, b, (((0,), (0,)), ((), ())), preferred_element_type=jnp.float32)


def nn(a, b):
    return lax.dot_general(a, b, (((1,), (0,)), ((), ())), preferred_element_type=jnp.float32)


def kernel(
    nctx, nx,
    slots, q_h, do_h, lse_h, delta_h, kv, kvin_h, feats_h,
    qg, kvg, wg,
    q, do, lse, delta, kvin, feats, kb, vb, prob, dv, dk, rdv, rdk, lt, vgb, vall, acc, odd_out, odd_in, even_out, even_in, fin, gat, lrow,
    s_in, s_kv, r_kv, s_part, r_part, s_l, r_l, r_core, s_v, r_v, s_odd, r_odd, s_even, r_even, s_f, r_f,
):
    ctx, head, p = lax.axis_index("ctx"), lax.axis_index("head"), lax.axis_index("dp")
    nz = nctx // 2
    np_ = nz // 2
    e, z = ctx // nz, ctx % nz
    yh, x = head // nx, head % nx
    S, dh = kb.shape[1], kb.shape[2]
    half = S // 2
    hq = q.shape[1] // dh
    F = feats.shape[1]
    scale = 1.0 / math.sqrt(dh)
    left, right = (ctx + nctx - 1) % nctx, (ctx + 1) % nctx
    mine = 2 * e + p
    xs = [(x + r) % nx for r in range(nx)]

    def dev(c=ctx, h=head, d=p):
        return (c, h, d)

    def at(e_=e, z_=z, y_=yh, x_=x, p_=p):
        return (e_ * nz + z_, y_ * nx + x_, p_)

    def send(src, dst, ss, rs, to):
        copy = pltpu.make_async_remote_copy(
            src_ref=src, dst_ref=dst, send_sem=ss, recv_sem=rs, device_id=to, device_id_type=MESH
        )
        copy.start()
        return copy

    def arrived(dst, rs):
        pltpu.make_async_remote_copy(
            src_ref=dst, dst_ref=dst, send_sem=rs, recv_sem=rs, device_id=dev(d=1 - p), device_id_type=MESH
        ).wait_recv()

    fetched = [
        pltpu.make_async_copy(src, dst, s_in.at[i])
        for i, (src, dst) in enumerate(
            ((feats_h, feats), (lse_h, lse), (q_h, q), (do_h, do), (delta_h, delta), (kvin_h, kvin))
        )
    ]
    for copy in fetched:
        copy.start()

    barrier = pltpu.get_barrier_semaphore()

    def greet(to):
        pl.semaphore_signal(barrier, inc=1, device_id=to, device_id_type=MESH)

    greet(dev(c=left))
    greet(dev(c=right))
    greet(at(z_=(z + 1) % nz))
    greet(at(z_=(z + nz - 1) % nz))
    greet(at(z_=(z + 2) % nz))
    greet(at(z_=(z + nz - 2) % nz))
    group = [(r, a, b) for r in range(nx) for a in (0, 1) for b in (0, 1) if (r, a, b) != (0, 0, 0)]

    def member(r, a, b):
        return (1 - e if a else e), xs[r], (1 - p if b else p)

    for r, a, b in group:
        e_, x_, p_ = member(r, a, b)
        greet(at(e_=e_, x_=x_, p_=p_))

    @pl.when(mine != yh)
    def _():
        for e_ in (0, 1):
            for p_ in (0, 1):
                greet(at(e_=e_, y_=mine, p_=p_))

    fetched[0].wait()
    lt[x, e, p] = feats[...].T
    fetched[1].wait()
    for side, blk in ((0, left), (1, right)):
        for kh in (0, 1):
            for qh in (0, 1):
                hidden = jnp.where(slots[2 * blk + kh] < slots[2 * ctx + qh], 0.0, 1e30).astype(jnp.float32)
                lanes = slice(qh * half, (qh + 1) * half)
                lrow[side, kh, :, lanes] = lse[:, lanes] * LOG2E + hidden

    pl.semaphore_wait(barrier, 6 + len(group) + NYH - 1)

    sends = []
    for part, buf in ((0, kb), (1, vb)):
        cols = slice(part * dh, (part + 1) * dh)
        for side, to in ((0, right), (1, left)):
            sends.append(send(kv.at[:, cols], buf.at[side], s_kv.at[part, side], r_kv.at[part, side], dev(c=to)))

    own = lt.at[x, e, p]
    hf = F // 2
    passed = []

    def pass_on(ref, sem, to):
        passed.append(send(ref, ref, s_l.at[len(passed)], sem, to))

    halves = (slice(0, hf), slice(hf, F))
    to_core, to_e = at(p_=1 - p), at(e_=1 - e)
    if nx > 1:
        xp, xm, xo = xs[1], xs[nx - 1], xs[2]
        to_xp, to_xm = at(x_=xp), at(x_=xm)
    for h in (0, 1):
        pass_on(own.at[halves[h]], r_l.at[0, h], to_e)
        if nx > 1:
            pass_on(own.at[halves[h]], r_l.at[1, h], to_xp)
            pass_on(own.at[halves[1 - h]], r_l.at[3, 1 - h], to_xm)
    pass_on(own, r_core.at[0, 0], to_core)

    def share_other():
        other = lt.at[x, 1 - e, p]
        for h in (0, 1):
            arrived(other.at[halves[h]], r_l.at[0, h])
            if nx > 1:
                pass_on(other.at[halves[h]], r_l.at[2, h], to_xp)
                pass_on(other.at[halves[h]], r_l.at[4, h], to_xm)
        pass_on(other, r_core.at[0, 1], to_core)

    def near_pair(a):
        e_ = 1 - e if a else e
        return lt.at[xm, e_, p], lt.at[xp, e_, p]

    def share_side(a):
        if nx > 1:
            low, high = near_pair(a)
            arrived(low.at[halves[0]], r_l.at[1 + a, 0])
            pass_on(low.at[halves[0]], r_l.at[5 + a, 0], to_xp)
            arrived(high.at[halves[1]], r_l.at[3 + a, 1])
            pass_on(high.at[halves[1]], r_l.at[7 + a, 1], to_xm)

    def share_near(a):
        if nx > 1:
            low, high = near_pair(a)
            arrived(low.at[halves[1]], r_l.at[1 + a, 1])
            pass_on(low, r_core.at[nx - 1, a], to_core)
            arrived(high.at[halves[0]], r_l.at[3 + a, 0])
            pass_on(high, r_core.at[1, a], to_core)

    def share_far(a):
        if nx > 1:
            far = lt.at[xo, 1 - e if a else e, p]
            arrived(far.at[halves[0]], r_l.at[5 + a, 0])
            arrived(far.at[halves[1]], r_l.at[7 + a, 1])
            pass_on(far, r_core.at[2, a], to_core)

    for copy in fetched[2:4]:
        copy.wait()
    heads = [slice(m * dh, (m + 1) * dh) for m in range(hq)]
    for side, to in ((0, left), (1, right)):
        arrived(kb.at[side], r_kv.at[0, side])
        total = None
        for m, lanes in enumerate(heads):
            st = nt(kb[side], q[:, lanes]) * (scale * LOG2E)
            st = st.reshape(2, half, S) - lrow[side, :, m : m + 1, :]
            pr = jnp.exp2(st).reshape(S, S)
            prob[m, side] = pr
            term = nn(pr.astype(jnp.bfloat16), do[:, lanes])
            total = term if total is None else total + term
        dv[side] = total
        sends.append(send(dv.at[side], rdv.at[side], s_part.at[0, side], r_part.at[0, side], dev(c=to)))

    share_other()
    share_side(0)

    for copy in fetched[4:]:
        copy.wait()
    for side in (0, 1):
        arrived(vb.at[side], r_kv.at[1, side])
    totals = [None, None]
    for m, lanes in enumerate(heads):
        qm, dom = q[:, lanes], do[:, lanes]
        whole = None
        for side in (0, 1):
            dots = nt(vb[side], dom) - delta[m : m + 1, :]
            ds = (prob[m, side] * dots).astype(jnp.bfloat16)
            term = nn(ds, qm)
            totals[side] = term if totals[side] is None else totals[side] + term
            term = tn(ds, kb[side])
            whole = term if whole is None else whole + term
        qg[:, lanes] = whole * scale
    for side, to in ((0, left), (1, right)):
        dk[side] = totals[side] * scale
        sends.append(send(dk.at[side], rdk.at[side], s_part.at[1, side], r_part.at[1, side], dev(c=to)))

    share_near(0)

    for side in (0, 1):
        arrived(rdv.at[side], r_part.at[0, side])
    new_v = kvin[:, dh:] + rdv[0] + rdv[1]
    kvg[:, dh:] = new_v
    vgb[...] = new_v.astype(jnp.bfloat16)
    te, tp = yh // 2, yh % 2
    for o in range(1, NYH):
        sends.append(send(vgb, vall.at[e, p], s_v.at[o], r_v.at[e, p], at(e_=te, y_=(yh + o) % NYH, p_=tp)))

    @pl.when(mine == yh)
    def _():
        vall[e, p] = vgb[...]

    @pl.when(mine != yh)
    def _():
        send(vgb, vall.at[e, p], s_v.at[0], r_v.at[e, p], at(e_=te, p_=tp))

    share_side(1)
    share_far(0)
    share_near(1)

    for side in (0, 1):
        arrived(rdk.at[side], r_part.at[1, side])
    kvg[:, :dh] = kvin[:, :dh] + rdk[0] + rdk[1]

    share_far(1)

    for e_ in (0, 1):
        for p_ in (0, 1):
            @pl.when((mine != yh) | (e_ != e) | (p_ != p))
            def _(e_=e_, p_=p_):
                arrived(vall.at[e_, p_], r_v.at[e_, p_])

    order = (0, nx - 1, 1, 2) if nx > 1 else (0,)
    ng = odd_in.shape[2]
    per = len(order) // ng
    kc = np_ // 2

    def blocks(g):
        return slice(g * per, (g + 1) * per)

    def term_for(g, d, k):
        to = (z + k) % nz if d == 0 else (z + nz - k) % nz
        return acc[blocks(g), :, to]

    def weight_term(i):
        r = order[i]
        for a in (0, 1):
            e_, x_, _ = member(r, a, 0)
            arrived(lt.at[x_, e_, 1 - p], r_core.at[r, a])
        total = None
        for e_ in (0, 1):
            for p_ in (0, 1):
                term = nn(lt[xs[r], e_, p_], vall[e_, p_])
                total = term if total is None else total + term
        acc[i] = total.reshape(acc.shape[1:])

    def next_odd(i, g, d):
        k = np_ - 1 - 2 * i
        odd_out[d, i, g] = term_for(g, d, k).astype(jnp.bfloat16)
        sends.append(send(odd_out.at[d, i, g], odd_in.at[d, i, g], s_odd.at[d, i, g], r_odd.at[d, i, g], beside[d]))

    def stop(i, g, d):
        k = np_ - 2 * i - (0 if d == 0 else 2)
        value = term_for(g, d, k)
        got = i - 1 if d == 0 else i
        if got >= 0:
            arrived(odd_in.at[d, got, g], r_odd.at[d, got, g])
            value = value + odd_in[d, got, g].astype(jnp.float32)
        if i > 0:
            arrived(even_in.at[d, i - 1, g], r_even.at[d, i - 1, g])
            value = value + even_in[d, i - 1, g].astype(jnp.float32)
        even_out[d, i, g] = value.astype(jnp.bfloat16)
        sends.append(
            send(even_out.at[d, i, g], even_in.at[d, i, g], s_even.at[d, i, g], r_even.at[d, i, g], beyond[d])
        )

    beside = (at(z_=(z + 1) % nz), at(z_=(z + nz - 1) % nz))
    beyond = (at(z_=(z + 2) % nz), at(z_=(z + nz - 2) % nz))
    for g in range(ng):
        for i in range(g * per, (g + 1) * per):
            weight_term(i)
        stop(0, g, 0)
        for i in range(kc):
            next_odd(i, g, 1)
            next_odd(i, g, 0)
    for i in range(kc):
        for g in range(ng):
            if i > 0:
                stop(i, g, 0)
            if i < kc - 1:
                stop(i, g, 1)

    for i, r in enumerate(order):
        g, k = i // per, i % per
        whole = acc[i, :, z]
        for d, n in ((0, kc), (1, kc - 1)):
            if k == 0:
                arrived(odd_in.at[d, kc - 1, g], r_odd.at[d, kc - 1, g])
            whole = whole + odd_in[d, kc - 1, g, k].astype(jnp.float32)
            if n > 0:
                if k == 0:
                    arrived(even_in.at[d, n - 1, g], r_even.at[d, n - 1, g])
                whole = whole + even_in[d, n - 1, g, k].astype(jnp.float32)
        fin[r] = whole.reshape(fin.shape[1:])
        for j, (r_, a, b) in enumerate(group):
            if r_ == r:
                e_, x_, p_ = member(r, a, b)
                col = mine * nx + x
                sends.append(
                    send(fin.at[r, e_, p_], gat.at[col], s_f.at[j], r_f.at[r, a, b], at(e_=e_, x_=x_, p_=p_))
                )
    gat[mine * nx + x] = fin[0, e, p]
    for r, a, b in group:
        e_, _, p_ = member(r, a, b)
        col = (2 * e_ + p_) * nx + xs[(nx - r) % nx]
        arrived(gat.at[col], r_f.at[r, a, b])
    for c in range(NYH * nx):
        wg[:, c * dh : (c + 1) * dh] = gat[c]

    for copy in sends + passed:
        copy.wait_send()

    @pl.when(mine != yh)
    def _():
        pltpu.make_async_remote_copy(
            src_ref=vgb, dst_ref=vall.at[e, p], send_sem=s_v.at[0], recv_sem=r_v.at[e, p],
            device_id=at(e_=te, p_=tp), device_id_type=MESH,
        ).wait_send()


def hand_over(a, b, c, a_out, b_out, c_out, a_here, b_here, c_here, sems):
    n = a.shape[0] // 4
    cuts = [slice(i * n, (i + 1) * n) for i in range(4)]
    moves = [(a.at[cut], a_here.at[cut], a_out.at[cut]) for cut in cuts]
    moves += [(b, b_here, b_out), (c, c_here, c_out)]
    steps = [
        (pltpu.make_async_copy(src, here, sems.at[0, i]), pltpu.make_async_copy(here, dst, sems.at[1, i]))
        for i, (src, here, dst) in enumerate(moves)
    ]
    for take, _ in steps:
        take.start()
    for take, give in steps:
        take.wait()
        give.start()
    for _, give in steps:
        give.wait()


def on_device(nctx, nx, query, out_grad, row_lse, row_delta, key_value, kv_grad_in, layer_input, slot_order):
    S, dh = query.shape[1], key_value.shape[2] // 2
    hq = query.shape[2] // dh
    F = layer_input.shape[2]
    nz = nctx // 2
    rows = F // (2 * nctx)
    kc = nz // 4
    f32, bf16 = jnp.float32, jnp.bfloat16
    vmem = pl.BlockSpec(memory_space=pltpu.VMEM)
    dma = pltpu.SemaphoreType.DMA
    ng = 2 if nx > 1 else 1
    piece = (ng, nx // ng, 2, 2 * rows, dh)
    outs = pl.pallas_call(
        functools.partial(kernel, nctx, nx),
        out_shape=(
            jax.ShapeDtypeStruct((S, hq * dh), f32),
            jax.ShapeDtypeStruct((S, 2 * dh), f32),
            jax.ShapeDtypeStruct((rows, NYH * nx * dh), f32),
        ),
        in_specs=[pl.BlockSpec(memory_space=pltpu.SMEM)] + [pl.BlockSpec(memory_space=pl.ANY)] * 7,
        out_specs=(vmem,) * 3,
        scratch_shapes=[
            pltpu.VMEM((S, hq * dh), bf16),
            pltpu.VMEM((S, hq * dh), bf16),
            pltpu.VMEM((hq, S), f32),
            pltpu.VMEM((hq, S), f32),
            pltpu.VMEM((S, 2 * dh), f32),
            pltpu.VMEM((S, F), bf16),
            pltpu.VMEM((2, S, dh), bf16),
            pltpu.VMEM((2, S, dh), bf16),
            pltpu.VMEM((hq, 2, S, S), f32),
            pltpu.VMEM((2, S, dh), f32),
            pltpu.VMEM((2, S, dh), f32),
            pltpu.VMEM((2, S, dh), f32),
            pltpu.VMEM((2, S, dh), f32),
            pltpu.VMEM((nx, 2, 2, F, S), bf16),
            pltpu.VMEM((S, dh), bf16),
            pltpu.VMEM((2, 2, S, dh), bf16),
            pltpu.VMEM((nx, 2, nz, 2 * rows, dh), f32),
            pltpu.VMEM((2, kc) + piece, bf16),
            pltpu.VMEM((2, kc) + piece, bf16),
            pltpu.VMEM((2, kc) + piece, bf16),
            pltpu.VMEM((2, kc) + piece, bf16),
            pltpu.VMEM((nx, 2, 2, rows, dh), f32),
            pltpu.VMEM((NYH * nx, rows, dh), f32),
            pltpu.VMEM((2, 2, hq, S), f32),
            dma((6,)), dma((2, 2)), dma((2, 2)), dma((2, 2)), dma((2, 2)),
            dma((32,)), dma((9, 2)), dma((nx, 2)),
            dma((4,)), dma((2, 2)),
            dma((2, kc, ng)), dma((2, kc, ng)), dma((2, kc, ng)), dma((2, kc, ng)),
            dma((16,)), dma((nx, 2, 2)),
        ],
        compiler_params=pltpu.CompilerParams(
            collective_id=0, has_side_effects=True, vmem_limit_bytes=58 * 1024 * 1024
        ),
        cost_estimate=pl.CostEstimate(flops=2_000_000_000, bytes_accessed=6_000_000, transcendentals=1_000_000),
    )(
        slot_order, query[0], out_grad[0], row_lse[0], row_delta[0], key_value[0], kv_grad_in[0], layer_input[0]
    )
    outs = pl.pallas_call(
        hand_over,
        out_shape=tuple(jax.ShapeDtypeStruct(o.shape, o.dtype) for o in outs),
        in_specs=[pl.BlockSpec(memory_space=pl.ANY)] * 3,
        out_specs=(pl.BlockSpec(memory_space=pl.ANY),) * 3,
        scratch_shapes=[pltpu.VMEM(o.shape, o.dtype) for o in outs] + [dma((2, 6))],
        compiler_params=pltpu.CompilerParams(vmem_limit_bytes=58 * 1024 * 1024),
    )(*outs)
    return outs[0][None], outs[1][None], outs[2][None]


def solution(mesh):
    nctx, nhead = mesh.shape["ctx"], mesh.shape["head"]
    in_specs = (
        P("dp", "ctx", "head"),
        P("dp", "ctx", "head"),
        P("dp", "head", "ctx"),
        P("dp", "head", "ctx"),
        P("dp", "ctx", "head"),
        P("dp", "ctx", "head"),
        P("dp", "ctx", "head"),
        P(),
    )
    out_specs = (P("dp", "ctx", "head"), P("dp", "ctx", "head"), P("head", ("ctx", "dp"), None))
    return jax.shard_map(
        functools.partial(on_device, nctx, nhead // NYH),
        mesh=mesh, in_specs=in_specs, out_specs=out_specs, check_vma=False,
    )
```

```python
import functools
import math

import jax
import jax.numpy as jnp
from jax import lax
from jax.experimental import pallas as pl
from jax.experimental.pallas import tpu as pltpu
from jax.sharding import PartitionSpec as P

MESH = pl.DeviceIdType.MESH
LOG2E = 1.0 / math.log(2.0)
NYH = 4


def nt(a, b):
    return lax.dot_general(a, b, (((1,), (1,)), ((), ())), preferred_element_type=jnp.float32)


def tn(a, b):
    return lax.dot_general(a, b, (((0,), (0,)), ((), ())), preferred_element_type=jnp.float32)


def nn(a, b):
    return lax.dot_general(a, b, (((1,), (0,)), ((), ())), preferred_element_type=jnp.float32)


def kernel(
    nctx, nx,
    slots, q_h, do_h, lse_h, delta_h, kv, kvin_h, feats_h,
    qg, kvg, wg,
    q, do, lse, delta, kvin, feats, kb, vb, prob, dv, dk, rdv, rdk, lt, vgb, vall, acc, odd_out, odd_in, even_out, even_in, fin, gat, lrow,
    s_in, s_kv, r_kv, s_part, r_part, s_l, r_l, r_core, s_v, r_v, s_odd, r_odd, s_even, r_even, s_f, r_f,
):
    ctx, head, p = lax.axis_index("ctx"), lax.axis_index("head"), lax.axis_index("dp")
    nz = nctx // 2
    np_ = nz // 2
    e, z = ctx // nz, ctx % nz
    yh, x = head // nx, head % nx
    S, dh = kb.shape[1], kb.shape[2]
    half = S // 2
    hq = q.shape[1] // dh
    F = feats.shape[1]
    scale = 1.0 / math.sqrt(dh)
    left, right = (ctx + nctx - 1) % nctx, (ctx + 1) % nctx
    mine = 2 * e + p
    xs = [(x + r) % nx for r in range(nx)]

    def dev(c=ctx, h=head, d=p):
        return (c, h, d)

    def at(e_=e, z_=z, y_=yh, x_=x, p_=p):
        return (e_ * nz + z_, y_ * nx + x_, p_)

    def send(src, dst, ss, rs, to):
        copy = pltpu.make_async_remote_copy(
            src_ref=src, dst_ref=dst, send_sem=ss, recv_sem=rs, device_id=to, device_id_type=MESH
        )
        copy.start()
        return copy

    def arrived(dst, rs):
        pltpu.make_async_remote_copy(
            src_ref=dst, dst_ref=dst, send_sem=rs, recv_sem=rs, device_id=dev(d=1 - p), device_id_type=MESH
        ).wait_recv()

    fetched = [
        pltpu.make_async_copy(src, dst, s_in.at[i])
        for i, (src, dst) in enumerate(
            ((feats_h, feats), (lse_h, lse), (q_h, q), (do_h, do), (delta_h, delta), (kvin_h, kvin))
        )
    ]
    for copy in fetched:
        copy.start()

    barrier = pltpu.get_barrier_semaphore()

    def greet(to):
        pl.semaphore_signal(barrier, inc=1, device_id=to, device_id_type=MESH)

    greet(dev(c=left))
    greet(dev(c=right))
    greet(at(z_=(z + 1) % nz))
    greet(at(z_=(z + nz - 1) % nz))
    greet(at(z_=(z + 2) % nz))
    greet(at(z_=(z + nz - 2) % nz))
    group = [(r, a, b) for r in range(nx) for a in (0, 1) for b in (0, 1) if (r, a, b) != (0, 0, 0)]

    def member(r, a, b):
        return (1 - e if a else e), xs[r], (1 - p if b else p)

    for r, a, b in group:
        e_, x_, p_ = member(r, a, b)
        greet(at(e_=e_, x_=x_, p_=p_))

    @pl.when(mine != yh)
    def _():
        for e_ in (0, 1):
            for p_ in (0, 1):
                greet(at(e_=e_, y_=mine, p_=p_))

    fetched[0].wait()
    lt[x, e, p] = feats[...].T
    fetched[1].wait()
    for side, blk in ((0, left), (1, right)):
        for kh in (0, 1):
            for qh in (0, 1):
                hidden = jnp.where(slots[2 * blk + kh] < slots[2 * ctx + qh], 0.0, 1e30).astype(jnp.float32)
                lanes = slice(qh * half, (qh + 1) * half)
                lrow[side, kh, :, lanes] = lse[:, lanes] * LOG2E + hidden

    pl.semaphore_wait(barrier, 6 + len(group) + NYH - 1)

    sends = []
    for part, buf in ((0, kb), (1, vb)):
        cols = slice(part * dh, (part + 1) * dh)
        for side, to in ((0, right), (1, left)):
            sends.append(send(kv.at[:, cols], buf.at[side], s_kv.at[part, side], r_kv.at[part, side], dev(c=to)))

    own = lt.at[x, e, p]
    hf = F // 2
    passed = []

    def pass_on(ref, sem, to):
        passed.append(send(ref, ref, s_l.at[len(passed)], sem, to))

    halves = (slice(0, hf), slice(hf, F))
    to_core, to_e = at(p_=1 - p), at(e_=1 - e)
    if nx > 1:
        xp, xm, xo = xs[1], xs[nx - 1], xs[2]
        to_xp, to_xm = at(x_=xp), at(x_=xm)
    for h in (0, 1):
        pass_on(own.at[halves[h]], r_l.at[0, h], to_e)
        if nx > 1:
            pass_on(own.at[halves[h]], r_l.at[1, h], to_xp)
            pass_on(own.at[halves[1 - h]], r_l.at[3, 1 - h], to_xm)
    pass_on(own, r_core.at[0, 0], to_core)

    def share_other():
        other = lt.at[x, 1 - e, p]
        for h in (0, 1):
            arrived(other.at[halves[h]], r_l.at[0, h])
            if nx > 1:
                pass_on(other.at[halves[h]], r_l.at[2, h], to_xp)
                pass_on(other.at[halves[h]], r_l.at[4, h], to_xm)
        pass_on(other, r_core.at[0, 1], to_core)

    def near_pair(a):
        e_ = 1 - e if a else e
        return lt.at[xm, e_, p], lt.at[xp, e_, p]

    def share_side(a):
        if nx > 1:
            low, high = near_pair(a)
            arrived(low.at[halves[0]], r_l.at[1 + a, 0])
            pass_on(low.at[halves[0]], r_l.at[5 + a, 0], to_xp)
            arrived(high.at[halves[1]], r_l.at[3 + a, 1])
            pass_on(high.at[halves[1]], r_l.at[7 + a, 1], to_xm)

    def share_near(a):
        if nx > 1:
            low, high = near_pair(a)
            arrived(low.at[halves[1]], r_l.at[1 + a, 1])
            pass_on(low, r_core.at[nx - 1, a], to_core)
            arrived(high.at[halves[0]], r_l.at[3 + a, 0])
            pass_on(high, r_core.at[1, a], to_core)

    def share_far(a):
        if nx > 1:
            far = lt.at[xo, 1 - e if a else e, p]
            arrived(far.at[halves[0]], r_l.at[5 + a, 0])
            arrived(far.at[halves[1]], r_l.at[7 + a, 1])
            pass_on(far, r_core.at[2, a], to_core)

    for copy in fetched[2:4]:
        copy.wait()
    heads = [slice(m * dh, (m + 1) * dh) for m in range(hq)]
    for side, to in ((0, left), (1, right)):
        arrived(kb.at[side], r_kv.at[0, side])
        total = None
        for m, lanes in enumerate(heads):
            st = nt(kb[side], q[:, lanes]) * (scale * LOG2E)
            st = st.reshape(2, half, S) - lrow[side, :, m : m + 1, :]
            pr = jnp.exp2(st).reshape(S, S)
            prob[m, side] = pr
            term = nn(pr.astype(jnp.bfloat16), do[:, lanes])
            total = term if total is None else total + term
        dv[side] = total
        sends.append(send(dv.at[side], rdv.at[side], s_part.at[0, side], r_part.at[0, side], dev(c=to)))

    share_other()
    share_side(0)

    for copy in fetched[4:]:
        copy.wait()
    for side in (0, 1):
        arrived(vb.at[side], r_kv.at[1, side])
    totals = [None, None]
    for m, lanes in enumerate(heads):
        qm, dom = q[:, lanes], do[:, lanes]
        whole = None
        for side in (0, 1):
            dots = nt(vb[side], dom) - delta[m : m + 1, :]
            ds = (prob[m, side] * dots).astype(jnp.bfloat16)
            term = nn(ds, qm)
            totals[side] = term if totals[side] is None else totals[side] + term
            term = tn(ds, kb[side])
            whole = term if whole is None else whole + term
        qg[:, lanes] = whole * scale
    for side, to in ((0, left), (1, right)):
        dk[side] = totals[side] * scale
        sends.append(send(dk.at[side], rdk.at[side], s_part.at[1, side], r_part.at[1, side], dev(c=to)))

    share_near(0)

    for side in (0, 1):
        arrived(rdv.at[side], r_part.at[0, side])
    new_v = kvin[:, dh:] + rdv[0] + rdv[1]
    kvg[:, dh:] = new_v
    vgb[...] = new_v.astype(jnp.bfloat16)
    te, tp = yh // 2, yh % 2
    for o in (2, 1, 3):
        sends.append(send(vgb, vall.at[e, p], s_v.at[o], r_v.at[e, p], at(e_=te, y_=(yh + o) % NYH, p_=tp)))

    @pl.when(mine == yh)
    def _():
        vall[e, p] = vgb[...]

    @pl.when(mine != yh)
    def _():
        send(vgb, vall.at[e, p], s_v.at[0], r_v.at[e, p], at(e_=te, p_=tp))

    share_side(1)
    share_far(0)
    share_near(1)

    for side in (0, 1):
        arrived(rdk.at[side], r_part.at[1, side])
    kvg[:, :dh] = kvin[:, :dh] + rdk[0] + rdk[1]

    share_far(1)

    for e_ in (0, 1):
        for p_ in (0, 1):
            @pl.when((mine != yh) | (e_ != e) | (p_ != p))
            def _(e_=e_, p_=p_):
                arrived(vall.at[e_, p_], r_v.at[e_, p_])

    order = (0, nx - 1, 1, 2) if nx > 1 else (0,)
    ng = odd_in.shape[2]
    per = len(order) // ng
    kc = np_ // 2

    def blocks(g):
        return slice(g * per, (g + 1) * per)

    def term_for(g, d, k):
        to = (z + k) % nz if d == 0 else (z + nz - k) % nz
        return acc[blocks(g), :, to]

    def weight_term(i):
        r = order[i]
        for a in (0, 1):
            e_, x_, _ = member(r, a, 0)
            arrived(lt.at[x_, e_, 1 - p], r_core.at[r, a])
        total = None
        for e_ in (0, 1):
            for p_ in (0, 1):
                term = nn(lt[xs[r], e_, p_], vall[e_, p_])
                total = term if total is None else total + term
        acc[i] = total.reshape(acc.shape[1:])

    def next_odd(i, g, d):
        k = np_ - 1 - 2 * i
        odd_out[d, i, g] = term_for(g, d, k).astype(jnp.bfloat16)
        sends.append(send(odd_out.at[d, i, g], odd_in.at[d, i, g], s_odd.at[d, i, g], r_odd.at[d, i, g], beside[d]))

    def stop(i, g, d):
        k = np_ - 2 * i - (0 if d == 0 else 2)
        value = term_for(g, d, k)
        got = i - 1 if d == 0 else i
        if got >= 0:
            arrived(odd_in.at[d, got, g], r_odd.at[d, got, g])
            value = value + odd_in[d, got, g].astype(jnp.float32)
        if i > 0:
            arrived(even_in.at[d, i - 1, g], r_even.at[d, i - 1, g])
            value = value + even_in[d, i - 1, g].astype(jnp.float32)
        even_out[d, i, g] = value.astype(jnp.bfloat16)
        sends.append(
            send(even_out.at[d, i, g], even_in.at[d, i, g], s_even.at[d, i, g], r_even.at[d, i, g], beyond[d])
        )

    beside = (at(z_=(z + 1) % nz), at(z_=(z + nz - 1) % nz))
    beyond = (at(z_=(z + 2) % nz), at(z_=(z + nz - 2) % nz))
    for g in range(ng):
        for i in range(g * per, (g + 1) * per):
            weight_term(i)
        stop(0, g, 0)
        next_odd(0, g, 1)
        next_odd(0, g, 0)
    for i in range(kc):
        if i + 1 < kc:
            for g in range(ng):
                next_odd(i + 1, g, 1)
        for g in range(ng):
            if i > 0:
                stop(i, g, 0)
            if i < kc - 1:
                stop(i, g, 1)
        if i + 1 < kc:
            for g in range(ng):
                next_odd(i + 1, g, 0)

    for i, r in enumerate(order):
        g, k = i // per, i % per
        whole = acc[i, :, z]
        for d, n in ((0, kc), (1, kc - 1)):
            if k == 0:
                arrived(odd_in.at[d, kc - 1, g], r_odd.at[d, kc - 1, g])
            whole = whole + odd_in[d, kc - 1, g, k].astype(jnp.float32)
            if n > 0:
                if k == 0:
                    arrived(even_in.at[d, n - 1, g], r_even.at[d, n - 1, g])
                whole = whole + even_in[d, n - 1, g, k].astype(jnp.float32)
        fin[r] = whole.reshape(fin.shape[1:])
        for j, (r_, a, b) in enumerate(group):
            if r_ == r:
                e_, x_, p_ = member(r, a, b)
                col = mine * nx + x
                sends.append(
                    send(fin.at[r, e_, p_], gat.at[col], s_f.at[j], r_f.at[r, a, b], at(e_=e_, x_=x_, p_=p_))
                )
    gat[mine * nx + x] = fin[0, e, p]
    for r, a, b in group:
        e_, _, p_ = member(r, a, b)
        col = (2 * e_ + p_) * nx + xs[(nx - r) % nx]
        arrived(gat.at[col], r_f.at[r, a, b])
    for c in range(NYH * nx):
        wg[:, c * dh : (c + 1) * dh] = gat[c]

    for copy in sends + passed:
        copy.wait_send()

    @pl.when(mine != yh)
    def _():
        pltpu.make_async_remote_copy(
            src_ref=vgb, dst_ref=vall.at[e, p], send_sem=s_v.at[0], recv_sem=r_v.at[e, p],
            device_id=at(e_=te, p_=tp), device_id_type=MESH,
        ).wait_send()


def hand_over(a, b, c, a_out, b_out, c_out, a_here, b_here, c_here, sems):
    n = a.shape[0] // 4
    cuts = [slice(i * n, (i + 1) * n) for i in range(4)]
    moves = [(a.at[cut], a_here.at[cut], a_out.at[cut]) for cut in cuts]
    moves += [(b, b_here, b_out), (c, c_here, c_out)]
    steps = [
        (pltpu.make_async_copy(src, here, sems.at[0, i]), pltpu.make_async_copy(here, dst, sems.at[1, i]))
        for i, (src, here, dst) in enumerate(moves)
    ]
    for take, _ in steps:
        take.start()
    for take, give in steps:
        take.wait()
        give.start()
    for _, give in steps:
        give.wait()


def on_device(nctx, nx, query, out_grad, row_lse, row_delta, key_value, kv_grad_in, layer_input, slot_order):
    S, dh = query.shape[1], key_value.shape[2] // 2
    hq = query.shape[2] // dh
    F = layer_input.shape[2]
    nz = nctx // 2
    rows = F // (2 * nctx)
    kc = nz // 4
    f32, bf16 = jnp.float32, jnp.bfloat16
    vmem = pl.BlockSpec(memory_space=pltpu.VMEM)
    dma = pltpu.SemaphoreType.DMA
    ng = 2 if nx > 1 else 1
    piece = (ng, nx // ng, 2, 2 * rows, dh)
    outs = pl.pallas_call(
        functools.partial(kernel, nctx, nx),
        out_shape=(
            jax.ShapeDtypeStruct((S, hq * dh), f32),
            jax.ShapeDtypeStruct((S, 2 * dh), f32),
            jax.ShapeDtypeStruct((rows, NYH * nx * dh), f32),
        ),
        in_specs=[pl.BlockSpec(memory_space=pltpu.SMEM)] + [pl.BlockSpec(memory_space=pl.ANY)] * 7,
        out_specs=(vmem,) * 3,
        scratch_shapes=[
            pltpu.VMEM((S, hq * dh), bf16),
            pltpu.VMEM((S, hq * dh), bf16),
            pltpu.VMEM((hq, S), f32),
            pltpu.VMEM((hq, S), f32),
            pltpu.VMEM((S, 2 * dh), f32),
            pltpu.VMEM((S, F), bf16),
            pltpu.VMEM((2, S, dh), bf16),
            pltpu.VMEM((2, S, dh), bf16),
            pltpu.VMEM((hq, 2, S, S), f32),
            pltpu.VMEM((2, S, dh), f32),
            pltpu.VMEM((2, S, dh), f32),
            pltpu.VMEM((2, S, dh), f32),
            pltpu.VMEM((2, S, dh), f32),
            pltpu.VMEM((nx, 2, 2, F, S), bf16),
            pltpu.VMEM((S, dh), bf16),
            pltpu.VMEM((2, 2, S, dh), bf16),
            pltpu.VMEM((nx, 2, nz, 2 * rows, dh), f32),
            pltpu.VMEM((2, kc) + piece, bf16),
            pltpu.VMEM((2, kc) + piece, bf16),
            pltpu.VMEM((2, kc) + piece, bf16),
            pltpu.VMEM((2, kc) + piece, bf16),
            pltpu.VMEM((nx, 2, 2, rows, dh), f32),
            pltpu.VMEM((NYH * nx, rows, dh), f32),
            pltpu.VMEM((2, 2, hq, S), f32),
            dma((6,)), dma((2, 2)), dma((2, 2)), dma((2, 2)), dma((2, 2)),
            dma((32,)), dma((9, 2)), dma((nx, 2)),
            dma((4,)), dma((2, 2)),
            dma((2, kc, ng)), dma((2, kc, ng)), dma((2, kc, ng)), dma((2, kc, ng)),
            dma((16,)), dma((nx, 2, 2)),
        ],
        compiler_params=pltpu.CompilerParams(
            collective_id=0, has_side_effects=True, vmem_limit_bytes=58 * 1024 * 1024
        ),
        cost_estimate=pl.CostEstimate(flops=2_000_000_000, bytes_accessed=6_000_000, transcendentals=1_000_000),
    )(
        slot_order, query[0], out_grad[0], row_lse[0], row_delta[0], key_value[0], kv_grad_in[0], layer_input[0]
    )
    outs = pl.pallas_call(
        hand_over,
        out_shape=tuple(jax.ShapeDtypeStruct(o.shape, o.dtype) for o in outs),
        in_specs=[pl.BlockSpec(memory_space=pl.ANY)] * 3,
        out_specs=(pl.BlockSpec(memory_space=pl.ANY),) * 3,
        scratch_shapes=[pltpu.VMEM(o.shape, o.dtype) for o in outs] + [dma((2, 6))],
        compiler_params=pltpu.CompilerParams(vmem_limit_bytes=58 * 1024 * 1024),
    )(*outs)
    return outs[0][None], outs[1][None], outs[2][None]


def solution(mesh):
    nctx, nhead = mesh.shape["ctx"], mesh.shape["head"]
    in_specs = (
        P("dp", "ctx", "head"),
        P("dp", "ctx", "head"),
        P("dp", "head", "ctx"),
        P("dp", "head", "ctx"),
        P("dp", "ctx", "head"),
        P("dp", "ctx", "head"),
        P("dp", "ctx", "head"),
        P(),
    )
    out_specs = (P("dp", "ctx", "head"), P("dp", "ctx", "head"), P("head", ("ctx", "dp"), None))
    return jax.shard_map(
        functools.partial(on_device, nctx, nhead // NYH),
        mesh=mesh, in_specs=in_specs, out_specs=out_specs, check_vma=False,
    )
```

```python
import functools
import math

import jax
import jax.numpy as jnp
from jax import lax
from jax.experimental import pallas as pl
from jax.experimental.pallas import tpu as pltpu
from jax.sharding import PartitionSpec as P

MESH = pl.DeviceIdType.MESH
LOG2E = 1.0 / math.log(2.0)
NYH = 4


def nt(a, b):
    return lax.dot_general(a, b, (((1,), (1,)), ((), ())), preferred_element_type=jnp.float32)


def tn(a, b):
    return lax.dot_general(a, b, (((0,), (0,)), ((), ())), preferred_element_type=jnp.float32)


def nn(a, b):
    return lax.dot_general(a, b, (((1,), (0,)), ((), ())), preferred_element_type=jnp.float32)


def kernel(
    nctx, nx,
    slots, q_h, do_h, lse_h, delta_h, kv, kvin_h, feats_h,
    qg, kvg, wg,
    q, do, lse, delta, kvin, feats, kb, vb, prob, dv, dk, rdv, rdk, lt, vgb, vall, acc, odd_out, odd_in, even_out, even_in, fin, gat, lrow,
    s_in, s_kv, r_kv, s_part, r_part, s_l, r_l, r_core, s_v, r_v, s_odd, r_odd, s_even, r_even, s_f, r_f,
):
    ctx, head, p = lax.axis_index("ctx"), lax.axis_index("head"), lax.axis_index("dp")
    nz = nctx // 2
    np_ = nz // 2
    e, z = ctx // nz, ctx % nz
    yh, x = head // nx, head % nx
    S, dh = kb.shape[1], kb.shape[2]
    half = S // 2
    hq = q.shape[1] // dh
    F = feats.shape[1]
    scale = 1.0 / math.sqrt(dh)
    left, right = (ctx + nctx - 1) % nctx, (ctx + 1) % nctx
    mine = 2 * e + p
    xs = [(x + r) % nx for r in range(nx)]

    def dev(c=ctx, h=head, d=p):
        return (c, h, d)

    def at(e_=e, z_=z, y_=yh, x_=x, p_=p):
        return (e_ * nz + z_, y_ * nx + x_, p_)

    def send(src, dst, ss, rs, to):
        copy = pltpu.make_async_remote_copy(
            src_ref=src, dst_ref=dst, send_sem=ss, recv_sem=rs, device_id=to, device_id_type=MESH
        )
        copy.start()
        return copy

    def arrived(dst, rs):
        pltpu.make_async_remote_copy(
            src_ref=dst, dst_ref=dst, send_sem=rs, recv_sem=rs, device_id=dev(d=1 - p), device_id_type=MESH
        ).wait_recv()

    fetched = [
        pltpu.make_async_copy(src, dst, s_in.at[i])
        for i, (src, dst) in enumerate(
            ((feats_h, feats), (lse_h, lse), (q_h, q), (do_h, do), (delta_h, delta), (kvin_h, kvin))
        )
    ]
    for copy in fetched:
        copy.start()

    barrier = pltpu.get_barrier_semaphore()

    def greet(to):
        pl.semaphore_signal(barrier, inc=1, device_id=to, device_id_type=MESH)

    greet(dev(c=left))
    greet(dev(c=right))
    greet(at(z_=(z + 1) % nz))
    greet(at(z_=(z + nz - 1) % nz))
    greet(at(z_=(z + 2) % nz))
    greet(at(z_=(z + nz - 2) % nz))
    group = [(r, a, b) for r in range(nx) for a in (0, 1) for b in (0, 1) if (r, a, b) != (0, 0, 0)]

    def member(r, a, b):
        return (1 - e if a else e), xs[r], (1 - p if b else p)

    for r, a, b in group:
        e_, x_, p_ = member(r, a, b)
        greet(at(e_=e_, x_=x_, p_=p_))

    @pl.when(mine != yh)
    def _():
        for e_ in (0, 1):
            for p_ in (0, 1):
                greet(at(e_=e_, y_=mine, p_=p_))

    fetched[0].wait()
    lt[x, e, p] = feats[...].T
    fetched[1].wait()
    for side, blk in ((0, left), (1, right)):
        for kh in (0, 1):
            for qh in (0, 1):
                hidden = jnp.where(slots[2 * blk + kh] < slots[2 * ctx + qh], 0.0, 1e30).astype(jnp.float32)
                lanes = slice(qh * half, (qh + 1) * half)
                lrow[side, kh, :, lanes] = lse[:, lanes] * LOG2E + hidden

    pl.semaphore_wait(barrier, 6 + len(group) + NYH - 1)

    sends = []
    for part, buf in ((0, kb), (1, vb)):
        cols = slice(part * dh, (part + 1) * dh)
        for side, to in ((0, right), (1, left)):
            sends.append(send(kv.at[:, cols], buf.at[side], s_kv.at[part, side], r_kv.at[part, side], dev(c=to)))

    own = lt.at[x, e, p]
    hf = F // 2
    passed = []

    def pass_on(ref, sem, to):
        passed.append(send(ref, ref, s_l.at[len(passed)], sem, to))

    halves = (slice(0, hf), slice(hf, F))
    to_core, to_e = at(p_=1 - p), at(e_=1 - e)
    if nx > 1:
        xp, xm, xo = xs[1], xs[nx - 1], xs[2]
        to_xp, to_xm = at(x_=xp), at(x_=xm)
    for h in (0, 1):
        pass_on(own.at[halves[h]], r_l.at[0, h], to_e)
        if nx > 1:
            pass_on(own.at[halves[h]], r_l.at[1, h], to_xp)
            pass_on(own.at[halves[1 - h]], r_l.at[3, 1 - h], to_xm)
    pass_on(own, r_core.at[0, 0], to_core)

    def share_other():
        other = lt.at[x, 1 - e, p]
        for h in (0, 1):
            arrived(other.at[halves[h]], r_l.at[0, h])
            if nx > 1:
                pass_on(other.at[halves[h]], r_l.at[2, h], to_xp)
                pass_on(other.at[halves[h]], r_l.at[4, h], to_xm)
        pass_on(other, r_core.at[0, 1], to_core)

    def near_pair(a):
        e_ = 1 - e if a else e
        return lt.at[xm, e_, p], lt.at[xp, e_, p]

    def share_side(a):
        if nx > 1:
            low, high = near_pair(a)
            arrived(low.at[halves[0]], r_l.at[1 + a, 0])
            pass_on(low.at[halves[0]], r_l.at[5 + a, 0], to_xp)
            arrived(high.at[halves[1]], r_l.at[3 + a, 1])
            pass_on(high.at[halves[1]], r_l.at[7 + a, 1], to_xm)

    def share_near(a):
        if nx > 1:
            low, high = near_pair(a)
            arrived(low.at[halves[1]], r_l.at[1 + a, 1])
            pass_on(low, r_core.at[nx - 1, a], to_core)
            arrived(high.at[halves[0]], r_l.at[3 + a, 0])
            pass_on(high, r_core.at[1, a], to_core)

    def share_far(a):
        if nx > 1:
            far = lt.at[xo, 1 - e if a else e, p]
            arrived(far.at[halves[0]], r_l.at[5 + a, 0])
            arrived(far.at[halves[1]], r_l.at[7 + a, 1])
            pass_on(far, r_core.at[2, a], to_core)

    for copy in fetched[2:4]:
        copy.wait()
    heads = [slice(m * dh, (m + 1) * dh) for m in range(hq)]
    for side, to in ((0, left), (1, right)):
        arrived(kb.at[side], r_kv.at[0, side])
        total = None
        for m, lanes in enumerate(heads):
            st = nt(kb[side], q[:, lanes]) * (scale * LOG2E)
            st = st.reshape(2, half, S) - lrow[side, :, m : m + 1, :]
            pr = jnp.exp2(st).reshape(S, S)
            prob[m, side] = pr
            term = nn(pr.astype(jnp.bfloat16), do[:, lanes])
            total = term if total is None else total + term
        dv[side] = total
        sends.append(send(dv.at[side], rdv.at[side], s_part.at[0, side], r_part.at[0, side], dev(c=to)))

    share_other()
    share_side(0)

    for copy in fetched[4:]:
        copy.wait()
    for side in (0, 1):
        arrived(vb.at[side], r_kv.at[1, side])
    totals = [None, None]
    for m, lanes in enumerate(heads):
        qm, dom = q[:, lanes], do[:, lanes]
        whole = None
        for side in (0, 1):
            dots = nt(vb[side], dom) - delta[m : m + 1, :]
            ds = (prob[m, side] * dots).astype(jnp.bfloat16)
            term = nn(ds, qm)
            totals[side] = term if totals[side] is None else totals[side] + term
            term = tn(ds, kb[side])
            whole = term if whole is None else whole + term
        qg[:, lanes] = whole * scale
    for side, to in ((0, left), (1, right)):
        dk[side] = totals[side] * scale
        sends.append(send(dk.at[side], rdk.at[side], s_part.at[1, side], r_part.at[1, side], dev(c=to)))

    share_near(0)

    for side in (0, 1):
        arrived(rdv.at[side], r_part.at[0, side])
    new_v = kvin[:, dh:] + rdv[0] + rdv[1]
    kvg[:, dh:] = new_v
    vgb[...] = new_v.astype(jnp.bfloat16)
    te, tp = yh // 2, yh % 2
    for o in (2, 1, 3):
        sends.append(send(vgb, vall.at[e, p], s_v.at[o], r_v.at[e, p], at(e_=te, y_=(yh + o) % NYH, p_=tp)))

    @pl.when(mine == yh)
    def _():
        vall[e, p] = vgb[...]

    @pl.when(mine != yh)
    def _():
        send(vgb, vall.at[e, p], s_v.at[0], r_v.at[e, p], at(e_=te, p_=tp))

    share_side(1)
    share_far(0)
    share_near(1)

    share_far(1)

    for e_ in (0, 1):
        for p_ in (0, 1):
            @pl.when((mine != yh) | (e_ != e) | (p_ != p))
            def _(e_=e_, p_=p_):
                arrived(vall.at[e_, p_], r_v.at[e_, p_])

    order = (0, nx - 1, 1, 2) if nx > 1 else (0,)
    ng = odd_in.shape[2]
    per = len(order) // ng
    kc = np_ // 2

    def blocks(g):
        return slice(g * per, (g + 1) * per)

    def term_for(g, d, k):
        to = (z + k) % nz if d == 0 else (z + nz - k) % nz
        return acc[blocks(g), :, to]

    def weight_term(i):
        r = order[i]
        for a in (0, 1):
            e_, x_, _ = member(r, a, 0)
            arrived(lt.at[x_, e_, 1 - p], r_core.at[r, a])
        total = None
        for e_ in (0, 1):
            for p_ in (0, 1):
                term = nn(lt[xs[r], e_, p_], vall[e_, p_])
                total = term if total is None else total + term
        acc[i] = total.reshape(acc.shape[1:])

    def next_odd(i, g, d):
        k = np_ - 1 - 2 * i
        odd_out[d, i, g] = term_for(g, d, k).astype(jnp.bfloat16)
        sends.append(send(odd_out.at[d, i, g], odd_in.at[d, i, g], s_odd.at[d, i, g], r_odd.at[d, i, g], beside[d]))

    def stop(i, g, d):
        k = np_ - 2 * i - (0 if d == 0 else 2)
        value = term_for(g, d, k)
        got = i - 1 if d == 0 else i
        if got >= 0:
            arrived(odd_in.at[d, got, g], r_odd.at[d, got, g])
            value = value + odd_in[d, got, g].astype(jnp.float32)
        if i > 0:
            arrived(even_in.at[d, i - 1, g], r_even.at[d, i - 1, g])
            value = value + even_in[d, i - 1, g].astype(jnp.float32)
        even_out[d, i, g] = value.astype(jnp.bfloat16)
        sends.append(
            send(even_out.at[d, i, g], even_in.at[d, i, g], s_even.at[d, i, g], r_even.at[d, i, g], beyond[d])
        )

    beside = (at(z_=(z + 1) % nz), at(z_=(z + nz - 1) % nz))
    beyond = (at(z_=(z + 2) % nz), at(z_=(z + nz - 2) % nz))
    for g in range(ng):
        for i in range(g * per, (g + 1) * per):
            weight_term(i)
        stop(0, g, 0)
        next_odd(0, g, 1)
        next_odd(0, g, 0)
    for i in range(kc):
        if i + 1 < kc:
            for g in range(ng):
                next_odd(i + 1, g, 1)
        for g in range(ng):
            if i > 0:
                stop(i, g, 0)
            if i < kc - 1:
                stop(i, g, 1)
        if i + 1 < kc:
            for g in range(ng):
                next_odd(i + 1, g, 0)

    for side in (0, 1):
        arrived(rdk.at[side], r_part.at[1, side])
    kvg[:, :dh] = kvin[:, :dh] + rdk[0] + rdk[1]

    for i, r in enumerate(order):
        g, k = i // per, i % per
        whole = acc[i, :, z]
        for d, n in ((0, kc), (1, kc - 1)):
            if k == 0:
                arrived(odd_in.at[d, kc - 1, g], r_odd.at[d, kc - 1, g])
            whole = whole + odd_in[d, kc - 1, g, k].astype(jnp.float32)
            if n > 0:
                if k == 0:
                    arrived(even_in.at[d, n - 1, g], r_even.at[d, n - 1, g])
                whole = whole + even_in[d, n - 1, g, k].astype(jnp.float32)
        fin[r] = whole.reshape(fin.shape[1:])
        for j, (r_, a, b) in enumerate(group):
            if r_ == r:
                e_, x_, p_ = member(r, a, b)
                col = mine * nx + x
                sends.append(
                    send(fin.at[r, e_, p_], gat.at[col], s_f.at[j], r_f.at[r, a, b], at(e_=e_, x_=x_, p_=p_))
                )
    gat[mine * nx + x] = fin[0, e, p]
    for r, a, b in group:
        e_, _, p_ = member(r, a, b)
        col = (2 * e_ + p_) * nx + xs[(nx - r) % nx]
        arrived(gat.at[col], r_f.at[r, a, b])
    for c in range(NYH * nx):
        wg[:, c * dh : (c + 1) * dh] = gat[c]

    for copy in sends + passed:
        copy.wait_send()

    @pl.when(mine != yh)
    def _():
        pltpu.make_async_remote_copy(
            src_ref=vgb, dst_ref=vall.at[e, p], send_sem=s_v.at[0], recv_sem=r_v.at[e, p],
            device_id=at(e_=te, p_=tp), device_id_type=MESH,
        ).wait_send()


def hand_over(a, b, c, a_out, b_out, c_out, a_here, b_here, c_here, sems):
    n = a.shape[0] // 4
    cuts = [slice(i * n, (i + 1) * n) for i in range(4)]
    moves = [(a.at[cut], a_here.at[cut], a_out.at[cut]) for cut in cuts]
    moves += [(b, b_here, b_out), (c, c_here, c_out)]
    steps = [
        (pltpu.make_async_copy(src, here, sems.at[0, i]), pltpu.make_async_copy(here, dst, sems.at[1, i]))
        for i, (src, here, dst) in enumerate(moves)
    ]
    for take, _ in steps:
        take.start()
    for take, give in steps:
        take.wait()
        give.start()
    for _, give in steps:
        give.wait()


def on_device(nctx, nx, query, out_grad, row_lse, row_delta, key_value, kv_grad_in, layer_input, slot_order):
    S, dh = query.shape[1], key_value.shape[2] // 2
    hq = query.shape[2] // dh
    F = layer_input.shape[2]
    nz = nctx // 2
    rows = F // (2 * nctx)
    kc = nz // 4
    f32, bf16 = jnp.float32, jnp.bfloat16
    vmem = pl.BlockSpec(memory_space=pltpu.VMEM)
    dma = pltpu.SemaphoreType.DMA
    ng = 2 if nx > 1 else 1
    piece = (ng, nx // ng, 2, 2 * rows, dh)
    outs = pl.pallas_call(
        functools.partial(kernel, nctx, nx),
        out_shape=(
            jax.ShapeDtypeStruct((S, hq * dh), f32),
            jax.ShapeDtypeStruct((S, 2 * dh), f32),
            jax.ShapeDtypeStruct((rows, NYH * nx * dh), f32),
        ),
        in_specs=[pl.BlockSpec(memory_space=pltpu.SMEM)] + [pl.BlockSpec(memory_space=pl.ANY)] * 7,
        out_specs=(vmem,) * 3,
        scratch_shapes=[
            pltpu.VMEM((S, hq * dh), bf16),
            pltpu.VMEM((S, hq * dh), bf16),
            pltpu.VMEM((hq, S), f32),
            pltpu.VMEM((hq, S), f32),
            pltpu.VMEM((S, 2 * dh), f32),
            pltpu.VMEM((S, F), bf16),
            pltpu.VMEM((2, S, dh), bf16),
            pltpu.VMEM((2, S, dh), bf16),
            pltpu.VMEM((hq, 2, S, S), f32),
            pltpu.VMEM((2, S, dh), f32),
            pltpu.VMEM((2, S, dh), f32),
            pltpu.VMEM((2, S, dh), f32),
            pltpu.VMEM((2, S, dh), f32),
            pltpu.VMEM((nx, 2, 2, F, S), bf16),
            pltpu.VMEM((S, dh), bf16),
            pltpu.VMEM((2, 2, S, dh), bf16),
            pltpu.VMEM((nx, 2, nz, 2 * rows, dh), f32),
            pltpu.VMEM((2, kc) + piece, bf16),
            pltpu.VMEM((2, kc) + piece, bf16),
            pltpu.VMEM((2, kc) + piece, bf16),
            pltpu.VMEM((2, kc) + piece, bf16),
            pltpu.VMEM((nx, 2, 2, rows, dh), f32),
            pltpu.VMEM((NYH * nx, rows, dh), f32),
            pltpu.VMEM((2, 2, hq, S), f32),
            dma((6,)), dma((2, 2)), dma((2, 2)), dma((2, 2)), dma((2, 2)),
            dma((32,)), dma((9, 2)), dma((nx, 2)),
            dma((4,)), dma((2, 2)),
            dma((2, kc, ng)), dma((2, kc, ng)), dma((2, kc, ng)), dma((2, kc, ng)),
            dma((16,)), dma((nx, 2, 2)),
        ],
        compiler_params=pltpu.CompilerParams(
            collective_id=0, has_side_effects=True, vmem_limit_bytes=58 * 1024 * 1024
        ),
        cost_estimate=pl.CostEstimate(flops=2_000_000_000, bytes_accessed=6_000_000, transcendentals=1_000_000),
    )(
        slot_order, query[0], out_grad[0], row_lse[0], row_delta[0], key_value[0], kv_grad_in[0], layer_input[0]
    )
    outs = pl.pallas_call(
        hand_over,
        out_shape=tuple(jax.ShapeDtypeStruct(o.shape, o.dtype) for o in outs),
        in_specs=[pl.BlockSpec(memory_space=pl.ANY)] * 3,
        out_specs=(pl.BlockSpec(memory_space=pl.ANY),) * 3,
        scratch_shapes=[pltpu.VMEM(o.shape, o.dtype) for o in outs] + [dma((2, 6))],
        compiler_params=pltpu.CompilerParams(vmem_limit_bytes=58 * 1024 * 1024),
    )(*outs)
    return outs[0][None], outs[1][None], outs[2][None]


def solution(mesh):
    nctx, nhead = mesh.shape["ctx"], mesh.shape["head"]
    in_specs = (
        P("dp", "ctx", "head"),
        P("dp", "ctx", "head"),
        P("dp", "head", "ctx"),
        P("dp", "head", "ctx"),
        P("dp", "ctx", "head"),
        P("dp", "ctx", "head"),
        P("dp", "ctx", "head"),
        P(),
    )
    out_specs = (P("dp", "ctx", "head"), P("dp", "ctx", "head"), P("head", ("ctx", "dp"), None))
    return jax.shard_map(
        functools.partial(on_device, nctx, nhead // NYH),
        mesh=mesh, in_specs=in_specs, out_specs=out_specs, check_vma=False,
    )
```
